256 devices in a mesh: gx: 16 (over x_lo, z), gy: 16 (over y, x_hi, core).
Axes of the slice: x: 4 (x_hi: 2, x_lo: 2; x = x_hi * 2 + x_lo), y: 4, z: 8, core: 2. Of those that a mesh axis runs over, the one named last changes fastest.
Arguments:
- features: bfloat16 [128, 128, 8, 128], P('gx', 'gy'), may hold values from -6 to 6
- weight_fine: bfloat16 [27, 128, 128], replicated, may hold values from -0.109375 to 0.109375
- weight_down: bfloat16 [27, 128, 256], replicated, may hold values from -0.109375 to 0.109375
- weight_mid: bfloat16 [27, 256, 256], replicated, may hold values from -0.078125 to 0.078125
- cotangent: bfloat16 [64, 64, 4, 256], P('gx', 'gy'), may hold values from -24 to 24
Outputs:
- grad_features: bfloat16 [128, 128, 8, 128], P('gx', 'gy')
- grad_fine: float32 [128, 27, 128], P('gx', None, 'gy')
- grad_down: float32 [128, 27, 256], P('gx', None, 'gy')
- grad_mid: float32 [256, 27, 256], P('gx', None, 'gy')
The draws below stay inside these ranges and needn't reach their ends.
All inputs are finite; a program needn't handle non-finite values.
Results may differ from the reference program's by a relative error of at most 0.014.
Values may be sent and summed in bfloat16 or wider, within the bound.
A program may use at most 128 MiB of HBM per device.

```python
import math
import jax
import jax.numpy as jnp
from jax import lax

C3 = 128
C4 = 256
X3 = 128
Y3 = 128
Z3 = 8
X4 = 64
Y4 = 64
Z4 = 4


def levels(stream_key, shape, cuts, least, largest):
    factor_of = 1.0
    for dim, parts in cuts:
        steps = jax.random.uniform(jax.random.fold_in(jax.random.fold_in(stream_key, 6), dim), (parts,), jnp.float32, least / len(cuts), largest / len(cuts))
        factor_of = factor_of * jnp.repeat(jnp.exp(steps), shape[dim] // parts).reshape((-1,) + (1,) * (len(shape) - 1 - dim))
    return factor_of


def bell_draw(stream_key, extent, spread, bound, cuts=(), dtype=jnp.bfloat16):
    loudness = levels(stream_key, extent, cuts, -0.22, 0.18) if cuts else 1.0
    values = jax.random.normal(stream_key, extent, jnp.float32) * spread * loudness
    return jnp.minimum(jnp.maximum(values, -bound), bound).astype(dtype)


def setup_inputs(seed: int = 0) -> dict:
    seeds = jax.random.split(jax.random.key(seed), 6)
    return {
        "features": bell_draw(seeds[0], (X3, Y3, Z3, C3), 1.0, 6.0, ((0, 16), (1, 16))),
        "weight_fine": bell_draw(seeds[1], (27, C3, C3), (27 * C3) ** -0.5, 0.109375),
        "weight_down": bell_draw(seeds[2], (27, C3, C4), (27 * C3) ** -0.5, 0.109375),
        "weight_mid": bell_draw(seeds[3], (27, C4, C4), (27 * C4) ** -0.5, 0.078125),
        "cotangent": bell_draw(seeds[4], (X4, Y4, Z4, C4), 4.0, 24.0, ((0, 16), (1, 16))),
    }


OFFSETS = [(i, j, k) for i in range(3) for j in range(3) for k in range(3)]
HIGH = lax.Precision.HIGHEST

def padded(field):
    return jnp.pad(field, ((1, 1), (1, 1), (1, 1), (0, 0)))

def convolve(field, weight):
    nx, ny, nz = (field.shape[0], field.shape[1], field.shape[2])
    ext = padded(field)
    total = jnp.zeros((nx, ny, nz, weight.shape[2]), jnp.float32)
    for index, (i, j, k) in enumerate(OFFSETS):
        total = total + jnp.einsum('xyzc,cd->xyzd', ext[i:i + nx, j:j + ny, k:k + nz], weight[index], precision=HIGH)
    return total

def adjoint(grad, weight):
    nx, ny, nz = (grad.shape[0], grad.shape[1], grad.shape[2])
    ext = padded(grad)
    total = jnp.zeros((nx, ny, nz, weight.shape[1]), jnp.float32)
    for index, (i, j, k) in enumerate(OFFSETS):
        total = total + jnp.einsum('xyzd,cd->xyzc', ext[2 - i:2 - i + nx, 2 - j:2 - j + ny, 2 - k:2 - k + nz], weight[index], precision=HIGH)
    return total

def weight_grad(field, grad):
    nx, ny, nz = (grad.shape[0], grad.shape[1], grad.shape[2])
    ext = padded(field)
    terms = [jnp.einsum('xyzc,xyzd->cd', ext[i:i + nx, j:j + ny, k:k + nz], grad, precision=HIGH) for i, j, k in OFFSETS]
    return jnp.stack(terms, axis=1)

def slope(pre):
    sig = jax.nn.sigmoid(pre)
    return sig * (1.0 + pre * (1.0 - sig))

def reference(features, weight_fine, weight_down, weight_mid, cotangent):
    feat = features.astype(jnp.float32)
    w_fine = weight_fine.astype(jnp.float32)
    w_down = weight_down.astype(jnp.float32)
    w_mid = weight_mid.astype(jnp.float32)
    pre_fine = convolve(feat, w_fine)
    act_fine = jax.nn.silu(pre_fine)
    pooled = act_fine.reshape(X4, 2, Y4, 2, Z4, 2, C3).mean(axis=(1, 3, 5)).astype(jnp.bfloat16)
    pooled_f = pooled.astype(jnp.float32)
    pre_coarse = convolve(pooled_f, w_down)
    act_coarse = jax.nn.silu(pre_coarse).astype(jnp.bfloat16)
    cot = cotangent.astype(jnp.float32)
    delta_act = adjoint(cot, w_mid)
    delta_coarse = (delta_act * slope(pre_coarse)).astype(jnp.bfloat16)
    delta_cf = delta_coarse.astype(jnp.float32)
    delta_pool = adjoint(delta_cf, w_down)
    spread_up = jnp.broadcast_to(delta_pool[:, None, :, None, :, None, :], (X4, 2, Y4, 2, Z4, 2, C3)).reshape(X3, Y3, Z3, C3)
    delta_fine = (spread_up * 0.125 * slope(pre_fine)).astype(jnp.bfloat16)
    delta_ff = delta_fine.astype(jnp.float32)
    grad_features = adjoint(delta_ff, w_fine).astype(jnp.bfloat16)
    fine_scale = math.sqrt(X3 * Y3 * Z3)
    coarse_scale = math.sqrt(X4 * Y4 * Z4)
    grad_fine = weight_grad(feat, delta_ff) / fine_scale
    grad_down = weight_grad(pooled_f, delta_cf) / coarse_scale
    grad_mid = weight_grad(act_coarse.astype(jnp.float32), cot) / coarse_scale
    return (grad_features, grad_fine, grad_down, grad_mid)
```

```python
import math

import jax
import jax.numpy as jnp
from jax import lax
from jax.experimental import pallas as pl
from jax.experimental.pallas import tpu as pltpu
from jax.sharding import PartitionSpec as P

MESH = pl.DeviceIdType.MESH
F32 = jnp.float32
BF16 = jnp.bfloat16

N = 16
BASE = 8
FX, FZ, C3 = 8, 8, 128
CX, CZ, C4 = 4, 4, 256
FR, CR = FX * FZ, CX * CZ
HALF = 14 * C3

FEAT, COT, POOL, DC, DF = range(5)
COT_T, POOL_G, ACT_G, DC_T, FINE, X_MID, X_DOWN, X_FINE = range(8)


def dot(a, b):
    return jnp.dot(a, b, preferred_element_type=F32)


def dot_t(a, b):
    return lax.dot_general(a, b, (((1,), (1,)), ((), ())), preferred_element_type=F32)


def own_rows(nz):
    return BASE + nz, BASE + nz + nz * (FX if nz == FZ else CX)


def put_own(ext, own, nz):
    lo, hi = own_rows(nz)
    nx = own.shape[0]
    ext[...] = jnp.zeros(ext.shape, F32)
    ext[1 : nx + 1, lo:hi, :] = own


def pack(ext, send_y, send_c, tmp, nz):
    lo, hi = own_rows(nz)
    nx = ext.shape[0] - 2
    chans = ext.shape[2]
    for side, start in ((0, lo), (1, hi - nz)):
        if nz == 8:
            send_y[side] = ext[1 : nx + 1, start : start + nz, :].reshape(nx * nz, chans).astype(BF16)
        else:
            for x in range(nx):
                tmp[side, nz * x : nz * x + nz, 0:chans] = ext[1 + x, start : start + nz, :]
            send_y[side] = tmp[side, 0 : nx * nz, 0:chans].astype(BF16)
        for end, x in ((0, 1), (1, nx)):
            send_c[2 * end + side] = ext[x, start : start + 16, :].astype(BF16)


def put_halo(ext, recv_x, recv_y, recv_c, inside, nz):
    lo, hi = own_rows(nz)
    nx = ext.shape[0] - 2
    chans = ext.shape[2]

    def kept(flag, value):
        return jnp.where(flag, value.astype(F32), 0.0)

    for end, x in ((0, 0), (1, nx + 1)):
        ext[x, lo:hi, :] = kept(inside[0][end], recv_x[end])
    for side, start in ((0, lo - nz), (1, hi)):
        line = kept(inside[1][side], recv_y[side])
        if nz == 8:
            ext[1 : nx + 1, start : start + nz, :] = line.reshape(nx, nz, chans)
        else:
            for x in range(nx):
                ext[1 + x, start : start + nz, :] = line[nz * x : nz * x + nz]
        for end, x in ((0, 0), (1, nx + 1)):
            flag = jnp.logical_and(inside[0][end], inside[1][side])
            ext[x, start : start + nz, :] = kept(flag, recv_c[2 * end + side])[0:nz]


def spread_lanes(ext, cols, nz):
    lo, hi = own_rows(nz)
    rows = hi - lo
    chans = ext.shape[2]
    z = lax.broadcasted_iota(jnp.int32, (rows, chans), 0) % nz

    def layer(x, carry):
        for b in range(3):
            for c in range(3):
                piece = ext[x, pl.ds(lo + nz * (b - 1) + c - 1, rows), :]
                if c == 0:
                    piece = jnp.where(z >= 1, piece, 0.0)
                if c == 2:
                    piece = jnp.where(z <= nz - 2, piece, 0.0)
                k = 3 * b + c
                cols[x, :, k * chans : (k + 1) * chans] = piece.astype(BF16)
        return carry

    lax.fori_loop(0, ext.shape[0], layer, 0)


def forward(cols, weight, nx):
    rows, depth = cols.shape[1], cols.shape[2]
    total = None
    for a in range(3):
        term = dot(
            cols[a : a + nx].reshape(nx * rows, depth),
            weight[9 * a : 9 * a + 9].reshape(depth, weight.shape[2]),
        )
        total = term if total is None else total + term
    return total


def backward(cols, weight, nx, total):
    rows = cols.shape[1]
    chans = weight.shape[2]
    for a in range(3):
        for k in range(9):
            piece = cols[a : a + nx, :, k * chans : (k + 1) * chans].reshape(nx * rows, chans)
            term = dot_t(piece, weight[26 - 9 * a - k])
            if a == 0 and k == 0:
                total[...] = term
            else:
                total[...] += term


def send_chunks(ext, flip, send_t):
    lo, hi = own_rows(CZ)
    flip[0:96, :] = ext[:, lo:hi, :].reshape(96, C4)
    flip[96:128, :] = jnp.zeros((32, C4), F32)
    send_t[...] = flip[...].T.astype(BF16)


def gather_lanes(recv_t, lines, shifted):
    lane = lax.broadcasted_iota(jnp.int32, (16, 128), 1) // 16
    for t in range(2):
        pieces = [recv_t[8 * t + s].astype(F32) for s in range(8)]
        for x in range(6):
            tile = jnp.zeros((16, 128), F32)
            for s in range(8):
                moved = pltpu.roll(pieces[s], (16 * s - 16 * x) % 128, 1) if s != x else pieces[s]
                tile = jnp.where(lane == s, moved, tile)
            lines[:, 256 * x + 128 * t : 256 * x + 128 * t + 128] = tile
    width = 6 * 256
    place = lax.broadcasted_iota(jnp.int32, (16, width), 1)
    z = place % CZ
    y = (place % 256) // CZ
    whole = lines[...]
    for b in range(3):
        for c in range(3):
            step = CZ * (b - 1) + c - 1
            moved = pltpu.roll(whole, (-step) % width, 1) if step else whole
            keep = (z + (c - 1) >= 0) & (z + (c - 1) < CZ) & (y + (b - 1) >= 0) & (y + (b - 1) < 64)
            k = 3 * b + c
            shifted[16 * k : 16 * k + 16, :] = jnp.where(keep, moved, 0.0).astype(BF16)


def coarse_grad(shifted, field, out):
    chans = field.shape[2]
    cells = field[...].reshape(1024, chans)
    out[432:512, 0:chans] = jnp.zeros((80, chans), F32)
    for a in range(3):
        term = dot(shifted[:, 256 * a : 256 * a + 1024], cells)
        for k in range(9):
            o = 26 - 9 * a - k
            out[16 * o : 16 * o + 16, 0:chans] = term[16 * k : 16 * k + 16]


def kernel(
    feat, cot, w_fine_hbm, w_down_hbm, w_mid_hbm,
    out_feat, out_fine, out_down, out_mid,
    w_fine, w_down, w_mid,
    ext_f, ext_c, ext_p, ext_d, ext_g,
    cols_f, cols_c, cols_p, cols_d, cols_g,
    own_p, own_d, own_g,
    sy_f, sc_f, rx_f, ry_f, rc_f,
    sy_c, sc_c, rx_c, ry_c, rc_c,
    sy_p, sc_p, rx_p, ry_p, rc_p,
    sy_d, sc_d, rx_d, ry_d, rc_d,
    sy_g, sc_g, rx_g, ry_g, rc_g,
    tmp, pairs, slope_f, delta_act, delta_pool, total_f,
    flip, lines, shifted_c, shifted_d, wide,
    st_c, rt_c, st_d, rt_d, all_p, all_a,
    part, send_f, recv_f, fold_f,
    sx_m, rx_m, sx_d, rx_d2, sx_f, rx_f2,
    w_sem, h_send, h_recv, a_send, a_recv,
):
    mx, my = lax.axis_index("gx"), lax.axis_index("gy")

    def other(axis, step):
        if axis == 0:
            return (lax.rem(mx + step, N), my)
        return (mx, lax.rem(my + step, N))

    loads = [
        pltpu.make_async_copy(src, dst, w_sem.at[i])
        for i, (src, dst) in enumerate(((w_fine_hbm, w_fine), (w_mid_hbm, w_mid), (w_down_hbm, w_down)))
    ]
    for load in loads:
        load.start()

    inside = ((mx > 0, mx < N - 1), (my > 0, my < N - 1))

    def neighbours(kind, first, last, send_y, send_c, recv_x, recv_y, recv_c):
        copies = []

        def add(src, dst, dx, dy):
            slot = len(copies)
            copies.append(
                pltpu.make_async_remote_copy(
                    src_ref=src,
                    dst_ref=dst,
                    send_sem=h_send.at[kind, slot],
                    recv_sem=h_recv.at[kind, slot],
                    device_id=(lax.rem(mx + dx + N, N), lax.rem(my + dy + N, N)),
                    device_id_type=MESH,
                )
            )

        add(first, recv_x.at[1], -1, 0)
        add(last, recv_x.at[0], 1, 0)
        for side in range(2):
            add(send_y.at[side], recv_y.at[1 - side], 0, 2 * side - 1)
        for end in range(2):
            for side in range(2):
                i = 2 * end + side
                add(send_c.at[i], recv_c.at[3 - i], 2 * end - 1, 2 * side - 1)
        return copies

    def exchange(kind, axis, src, dst):
        me = (mx, my)[axis]

        def copy(d, slot):
            return pltpu.make_async_remote_copy(
                src_ref=src(lax.rem(me + d, N)),
                dst_ref=dst(slot),
                send_sem=a_send.at[kind, d],
                recv_sem=a_recv.at[kind, d],
                device_id=other(axis, d),
                device_id_type=MESH,
            )

        def start():
            def body(d, carry):
                copy(d, me).start()
                return carry

            lax.fori_loop(1, N, body, 0)

        def arrive():
            def body(d, carry):
                copy(d, lax.rem(me - d + N, N)).wait_recv()
                return carry

            lax.fori_loop(1, N, body, 0)

        def leave():
            def body(d, carry):
                copy(d, me).wait_send()
                return carry

            lax.fori_loop(1, N, body, 0)

        return start, arrive, leave

    def sixteen(i):
        return pl.ds(pl.multiple_of(16 * i, 16), 16)

    halo_f = neighbours(FEAT, feat.at[0], feat.at[FX - 1], sy_f, sc_f, rx_f, ry_f, rc_f)
    halo_c = neighbours(COT, cot.at[0], cot.at[CX - 1], sy_c, sc_c, rx_c, ry_c, rc_c)
    halo_p = neighbours(POOL, own_p.at[0], own_p.at[CX - 1], sy_p, sc_p, rx_p, ry_p, rc_p)
    halo_d = neighbours(DC, own_d.at[0], own_d.at[CX - 1], sy_d, sc_d, rx_d, ry_d, rc_d)
    halo_g = neighbours(DF, own_g.at[0], own_g.at[FX - 1], sy_g, sc_g, rx_g, ry_g, rc_g)
    move_ct = exchange(COT_T, 1, lambda t: st_c.at[sixteen(t)], lambda s: rt_c.at[s])
    move_dt = exchange(DC_T, 1, lambda t: st_d.at[sixteen(t)], lambda s: rt_d.at[s])
    move_p = exchange(POOL_G, 1, lambda t: all_p.at[:, sixteen(my)], lambda s: all_p.at[:, sixteen(s)])
    move_a = exchange(ACT_G, 1, lambda t: all_a.at[:, sixteen(my)], lambda s: all_a.at[:, sixteen(s)])
    move_f = exchange(FINE, 1, lambda t: send_f.at[t], lambda s: recv_f.at[s])
    move_xm = exchange(X_MID, 0, lambda t: sx_m.at[t], lambda s: rx_m.at[s])
    move_xd = exchange(X_DOWN, 0, lambda t: sx_d.at[t], lambda s: rx_d2.at[s])
    move_xf = exchange(X_FINE, 0, lambda t: sx_f.at[t], lambda s: rx_f2.at[s])

    put_own(ext_f, feat[...].astype(F32), FZ)
    pack(ext_f, sy_f, sc_f, tmp, FZ)
    put_own(ext_c, cot[...].astype(F32), CZ)
    pack(ext_c, sy_c, sc_c, tmp, CZ)

    barrier = pltpu.get_barrier_semaphore()

    def greet(d, carry):
        for axis in range(2):
            pl.semaphore_signal(barrier, inc=1, device_id=other(axis, d), device_id_type=MESH)
        return carry

    lax.fori_loop(1, N, greet, 0)
    for dx in (1, N - 1):
        for dy in (1, N - 1):
            there = (lax.rem(mx + dx, N), lax.rem(my + dy, N))
            pl.semaphore_signal(barrier, inc=1, device_id=there, device_id_type=MESH)
    pl.semaphore_wait(barrier, 2 * (N - 1) + 4)

    for copy in halo_f + halo_c:
        copy.start()

    for copy in halo_f:
        copy.wait_recv()
    put_halo(ext_f, rx_f, ry_f, rc_f, inside, FZ)
    spread_lanes(ext_f, cols_f, FZ)
    loads[0].wait()
    pre = forward(cols_f, w_fine, FX)
    sig = jax.nn.sigmoid(pre)
    slope_f[...] = sig * (1.0 + pre * (1.0 - sig))
    act = (pre * sig).reshape(CX, 2, CX, 2, FZ, C3)
    pairs[...] = (act[:, 0, :, 0] + act[:, 0, :, 1] + act[:, 1, :, 0] + act[:, 1, :, 1]).reshape(128, C3)
    pooled = (pairs[pl.ds(0, 64, stride=2), :] + pairs[pl.ds(1, 64, stride=2), :]) * 0.125
    pooled = pooled.astype(BF16).reshape(CX, CR, C3)
    own_p[...] = pooled
    put_own(ext_p, pooled.astype(F32), CZ)
    pack(ext_p, sy_p, sc_p, tmp, CZ)
    for copy in halo_p:
        copy.start()
    all_p[:, sixteen(my), :] = pooled
    move_p[0]()

    for copy in halo_c:
        copy.wait_recv()
    put_halo(ext_c, rx_c, ry_c, rc_c, inside, CZ)
    send_chunks(ext_c, flip, st_c)
    move_ct[0]()
    rt_c[my] = st_c[sixteen(my), :]
    spread_lanes(ext_c, cols_c, CZ)
    loads[1].wait()
    backward(cols_c, w_mid, CX, delta_act)

    for copy in halo_p:
        copy.wait_recv()
    put_halo(ext_p, rx_p, ry_p, rc_p, inside, CZ)
    spread_lanes(ext_p, cols_p, CZ)
    loads[2].wait()
    pre = forward(cols_p, w_down, CX)
    sig = jax.nn.sigmoid(pre)
    delta = (delta_act[...] * (sig * (1.0 + pre * (1.0 - sig)))).astype(BF16).reshape(CX, CR, C4)
    own_d[...] = delta
    put_own(ext_d, delta.astype(F32), CZ)
    pack(ext_d, sy_d, sc_d, tmp, CZ)
    for copy in halo_d:
        copy.start()
    all_a[:, sixteen(my), :] = (pre * sig).astype(BF16).reshape(CX, CR, C4)
    move_a[0]()
    move_ct[1]()
    gather_lanes(rt_c, lines, shifted_c)

    for copy in halo_d:
        copy.wait_recv()
    put_halo(ext_d, rx_d, ry_d, rc_d, inside, CZ)
    spread_lanes(ext_d, cols_d, CZ)
    backward(cols_d, w_down, CX, delta_pool)
    pooled_delta = delta_pool[...] * 0.125
    pairs[pl.ds(0, 64, stride=2), :] = pooled_delta
    pairs[pl.ds(1, 64, stride=2), :] = pooled_delta
    up = jnp.broadcast_to(pairs[...].reshape(CX, 1, CX, 1, FZ, C3), (CX, 2, CX, 2, FZ, C3))
    delta = (up.reshape(512, C3) * slope_f[...]).astype(BF16)
    own_g[...] = delta.reshape(FX, FR, C3)
    put_own(ext_g, delta.astype(F32).reshape(FX, FR, C3), FZ)
    pack(ext_g, sy_g, sc_g, tmp, FZ)
    for copy in halo_g:
        copy.start()

    turned = ext_g[1 : FX + 1, BASE + FZ : BASE + FZ + FR, :].reshape(512, C3).T.astype(BF16)
    for a in range(3):
        part[:, 1152 * a : 1152 * a + 1152] = dot(turned, cols_f[a : a + FX].reshape(512, 1152))
    part[:, 27 * C3 : 28 * C3] = jnp.zeros((C3, C3), F32)

    def fold(j, carry):
        rows = pl.ds(pl.multiple_of(8 * j, 8), 8)
        send_f[j] = jnp.concatenate([part[rows, 0:HALF], part[rows, HALF : 2 * HALF]], axis=0).astype(BF16)
        return carry

    lax.fori_loop(0, N, fold, 0)
    move_f[0]()
    recv_f[my] = send_f[my]

    send_chunks(ext_d, flip, st_d)
    move_dt[0]()
    rt_d[my] = st_d[sixteen(my), :]

    move_a[1]()
    coarse_grad(shifted_c, all_a, wide)
    sx_m[...] = wide[...].T.astype(BF16).reshape(N, 16, 512)
    move_xm[0]()
    rx_m[mx] = sx_m[mx]

    for copy in halo_g:
        copy.wait_recv()
    put_halo(ext_g, rx_g, ry_g, rc_g, inside, FZ)
    spread_lanes(ext_g, cols_g, FZ)
    backward(cols_g, w_fine, FX, total_f)
    out_feat[...] = total_f[...].astype(BF16).reshape(FX, FR, C3)

    move_dt[1]()
    gather_lanes(rt_d, lines, shifted_d)
    move_p[1]()
    coarse_grad(shifted_d, all_p, wide)
    turned = wide[:, 0:C3].T
    for i in range(N):
        rows = turned[8 * i : 8 * i + 8]
        sx_d[i] = jnp.concatenate([rows[:, 0:256], rows[:, 256:512]], axis=0).astype(BF16)
    move_xd[0]()
    rx_d2[mx] = sx_d[mx]

    move_f[1]()

    def add_f(s, total):
        return total + recv_f[s].astype(F32)

    total = lax.fori_loop(0, N, add_f, jnp.zeros((16, HALF), F32))
    for o in range(28):
        half, at = divmod(o, 14)
        fold_f[8 * o : 8 * o + 8, :] = total[8 * half : 8 * half + 8, C3 * at : C3 * at + C3]
    fold_f[224:256, :] = jnp.zeros((32, C3), F32)
    turned = fold_f[...].T
    for i in range(N):
        rows = turned[8 * i : 8 * i + 8]
        sx_f[i] = jnp.concatenate([rows[:, 0:128], rows[:, 128:256]], axis=0).astype(BF16)
    move_xf[0]()
    rx_f2[mx] = sx_f[mx]

    def summed(arrived):
        def add(s, total):
            return total + arrived[s].astype(F32)

        return lax.fori_loop(0, N, add, jnp.zeros(arrived.shape[1:], F32))

    move_xm[1]()
    out_mid[...] = summed(rx_m) * (1.0 / math.sqrt(CX * N * CX * N * CZ))
    move_xd[1]()
    total = summed(rx_d2) * (1.0 / math.sqrt(CX * N * CX * N * CZ))
    out_down[:, 0:256] = total[0:8]
    out_down[:, 256:512] = total[8:16]
    move_xf[1]()
    total = summed(rx_f2) * (1.0 / math.sqrt(FX * N * FX * N * FZ))
    out_fine[:, 0:128] = total[0:8]
    out_fine[:, 128:256] = total[8:16]

    for copy in halo_f + halo_c + halo_p + halo_d + halo_g:
        copy.wait_send()
    for move in (move_ct, move_dt, move_p, move_a, move_f, move_xm, move_xd, move_xf):
        move[2]()


def halo_scratch(nx, rows, chans):
    lines = nx * rows // nx
    return [
        pltpu.VMEM((2, lines, chans), BF16),
        pltpu.VMEM((4, 16, chans), BF16),
        pltpu.VMEM((2, rows, chans), BF16),
        pltpu.VMEM((2, lines, chans), BF16),
        pltpu.VMEM((4, 16, chans), BF16),
    ]


def per_device(features, weight_fine, weight_down, weight_mid, cotangent):
    vmem = pl.BlockSpec(memory_space=pltpu.VMEM)
    anywhere = pl.BlockSpec(memory_space=pl.ANY)
    fine_ext = pltpu.VMEM((FX + 2, 2 * BASE + FZ * (FX + 2), C3), F32)
    fine_cols = pltpu.VMEM((FX + 2, FR, 9 * C3), BF16)

    def coarse_ext(chans):
        return pltpu.VMEM((CX + 2, 2 * BASE + CZ * (CX + 2), chans), F32)

    def coarse_cols(chans):
        return pltpu.VMEM((CX + 2, CR, 9 * chans), BF16)

    scratch = [
        pltpu.VMEM((27, C3, C3), BF16),
        pltpu.VMEM((27, C3, C4), BF16),
        pltpu.VMEM((27, C4, C4), BF16),
        fine_ext, coarse_ext(C4), coarse_ext(C3), coarse_ext(C4), fine_ext,
        fine_cols, coarse_cols(C4), coarse_cols(C3), coarse_cols(C4), fine_cols,
        pltpu.VMEM((CX, CR, C3), BF16),
        pltpu.VMEM((CX, CR, C4), BF16),
        pltpu.VMEM((FX, FR, C3), BF16),
        *halo_scratch(FX, FR, C3),
        *halo_scratch(CX, CR, C4),
        *halo_scratch(CX, CR, C3),
        *halo_scratch(CX, CR, C4),
        *halo_scratch(FX, FR, C3),
        pltpu.VMEM((2, 16, C4), F32),
        pltpu.VMEM((128, C3), F32),
        pltpu.VMEM((512, C3), F32),
        pltpu.VMEM((64, C4), F32),
        pltpu.VMEM((64, C3), F32),
        pltpu.VMEM((512, C3), F32),
        pltpu.VMEM((128, C4), F32),
        pltpu.VMEM((16, 6 * 256), F32),
        pltpu.VMEM((144, 6 * 256), BF16),
        pltpu.VMEM((144, 6 * 256), BF16),
        pltpu.VMEM((512, C4), F32),
        pltpu.VMEM((C4, 128), BF16),
        pltpu.VMEM((N, 16, 128), BF16),
        pltpu.VMEM((C4, 128), BF16),
        pltpu.VMEM((N, 16, 128), BF16),
        pltpu.VMEM((CX, N * CR, C3), BF16),
        pltpu.VMEM((CX, N * CR, C4), BF16),
        pltpu.VMEM((C3, 2 * HALF), F32),
        pltpu.VMEM((N, 16, HALF), BF16),
        pltpu.VMEM((N, 16, HALF), BF16),
        pltpu.VMEM((256, C3), F32),
        pltpu.VMEM((N, 16, 512), BF16),
        pltpu.VMEM((N, 16, 512), BF16),
        pltpu.VMEM((N, 16, 256), BF16),
        pltpu.VMEM((N, 16, 256), BF16),
        pltpu.VMEM((N, 16, 128), BF16),
        pltpu.VMEM((N, 16, 128), BF16),
        pltpu.SemaphoreType.DMA((3,)),
        pltpu.SemaphoreType.DMA((5, 8)),
        pltpu.SemaphoreType.DMA((5, 8)),
        pltpu.SemaphoreType.DMA((8, N)),
        pltpu.SemaphoreType.DMA((8, N)),
    ]
    out_feat, out_fine, out_down, out_mid = pl.pallas_call(
        kernel,
        out_shape=(
            jax.ShapeDtypeStruct((FX, FR, C3), BF16),
            jax.ShapeDtypeStruct((8, 256), F32),
            jax.ShapeDtypeStruct((8, 512), F32),
            jax.ShapeDtypeStruct((16, 512), F32),
        ),
        in_specs=[vmem, vmem, anywhere, anywhere, anywhere],
        out_specs=(vmem, vmem, vmem, vmem),
        scratch_shapes=scratch,
        compiler_params=pltpu.CompilerParams(
            collective_id=0, has_side_effects=True, vmem_limit_bytes=48 * 1024 * 1024
        ),
        name="unet_backward",
    )(
        features.reshape(FX, FR, C3),
        cotangent.reshape(CX, CR, C4),
        weight_fine,
        weight_down,
        weight_mid,
    )
    return (
        out_feat.reshape(FX, FX, FZ, C3),
        out_fine[:, : 27 * 8].reshape(8, 27, 8),
        out_down[:, : 27 * 16].reshape(8, 27, 16),
        out_mid[:, : 27 * 16].reshape(16, 27, 16),
    )


def solution(mesh):
    in_specs = (P("gx", "gy", None, None), P(), P(), P(), P("gx", "gy", None, None))
    out_specs = (
        P("gx", "gy", None, None),
        P("gx", None, "gy"),
        P("gx", None, "gy"),
        P("gx", None, "gy"),
    )
    return jax.shard_map(
        per_device, mesh=mesh, in_specs=in_specs, out_specs=out_specs, check_vma=False
    )
```

```python
import math

import jax
import jax.numpy as jnp
from jax import lax
from jax.experimental import pallas as pl
from jax.experimental.pallas import tpu as pltpu
from jax.sharding import PartitionSpec as P

MESH = pl.DeviceIdType.MESH
F32 = jnp.float32
BF16 = jnp.bfloat16

N = 16
BASE = 8
FX, FZ, C3 = 8, 8, 128
CX, CZ, C4 = 4, 4, 256
FR, CR = FX * FZ, CX * CZ
HALF = 7 * C3

FEAT, COT, POOL, DC, DF = range(5)
COT_T, POOL_G, ACT_G, DC_T, FINE, X_MID, X_DOWN, X_FINE = range(8)


def dot(a, b):
    return jnp.dot(a, b, preferred_element_type=F32)


def dot_t(a, b):
    return lax.dot_general(a, b, (((1,), (1,)), ((), ())), preferred_element_type=F32)


def own_rows(nz):
    return BASE + nz, BASE + nz + nz * (FX if nz == FZ else CX)


def put_own(ext, own, nz):
    lo, hi = own_rows(nz)
    nx = own.shape[0]
    ext[1 : nx + 1, lo:hi, :] = own


def pack(ext, send_y, send_c, tmp, nz):
    lo, hi = own_rows(nz)
    nx = ext.shape[0] - 2
    chans = ext.shape[2]
    for side, start in ((0, lo), (1, hi - nz)):
        if nz == 8:
            send_y[side] = ext[1 : nx + 1, start : start + nz, :].reshape(nx * nz, chans).astype(BF16)
        else:
            for x in range(nx):
                tmp[side, nz * x : nz * x + nz, 0:chans] = ext[1 + x, start : start + nz, :]
            send_y[side] = tmp[side, 0 : nx * nz, 0:chans].astype(BF16)
        for end, x in ((0, 1), (1, nx)):
            send_c[2 * end + side] = ext[x, start : start + 16, :].astype(BF16)


def put_halo(ext, recv_x, recv_y, recv_c, inside, nz):
    lo, hi = own_rows(nz)
    nx = ext.shape[0] - 2
    chans = ext.shape[2]

    def kept(flag, value):
        return jnp.where(flag, value.astype(F32), 0.0)

    for end, x in ((0, 0), (1, nx + 1)):
        ext[x, lo:hi, :] = kept(inside[0][end], recv_x[end])
    for side, start in ((0, lo - nz), (1, hi)):
        line = kept(inside[1][side], recv_y[side])
        if nz == 8:
            ext[1 : nx + 1, start : start + nz, :] = line.reshape(nx, nz, chans)
        else:
            for x in range(nx):
                ext[1 + x, start : start + nz, :] = line[nz * x : nz * x + nz]
        for end, x in ((0, 0), (1, nx + 1)):
            flag = jnp.logical_and(inside[0][end], inside[1][side])
            ext[x, start : start + nz, :] = kept(flag, recv_c[2 * end + side])[0:nz]


def spread_lanes(ext, cols, nz):
    lo, hi = own_rows(nz)
    rows = hi - lo
    chans = ext.shape[2]
    z = lax.broadcasted_iota(jnp.int32, (rows, chans), 0) % nz

    def layer(x, carry):
        for b in range(3):
            for c in range(3):
                piece = ext[x, pl.ds(lo + nz * (b - 1) + c - 1, rows), :]
                if c == 0:
                    piece = jnp.where(z >= 1, piece, 0.0)
                if c == 2:
                    piece = jnp.where(z <= nz - 2, piece, 0.0)
                k = 3 * b + c
                cols[x, :, k * chans : (k + 1) * chans] = piece.astype(BF16)
        return carry

    lax.fori_loop(0, ext.shape[0], layer, 0)


def forward(cols, weight, nx):
    rows, depth = cols.shape[1], cols.shape[2]
    total = None
    for a in range(3):
        term = dot(
            cols[a : a + nx].reshape(nx * rows, depth),
            weight[9 * a : 9 * a + 9].reshape(depth, weight.shape[2]),
        )
        total = term if total is None else total + term
    return total


def backward(cols, weight, nx, total):
    rows = cols.shape[1]
    chans = weight.shape[2]
    for a in range(3):
        for k in range(9):
            piece = cols[a : a + nx, :, k * chans : (k + 1) * chans].reshape(nx * rows, chans)
            term = dot_t(piece, weight[26 - 9 * a - k])
            if a == 0 and k == 0:
                total[...] = term
            else:
                total[...] += term


def send_chunks(ext, flip, send_t):
    lo, hi = own_rows(CZ)
    flip[0:96, :] = ext[:, lo:hi, :].reshape(96, C4)
    send_t[...] = flip[...].T.astype(BF16)


def gather_lanes(recv_t, lines, shifted):
    lane = lax.broadcasted_iota(jnp.int32, (16, 128), 1) // 16
    for t in range(2):
        pieces = [recv_t[8 * t + s].astype(F32) for s in range(8)]
        for x in range(6):
            tile = jnp.zeros((16, 128), F32)
            for s in range(8):
                moved = pltpu.roll(pieces[s], (16 * s - 16 * x) % 128, 1) if s != x else pieces[s]
                tile = jnp.where(lane == s, moved, tile)
            lines[:, 256 * x + 128 * t : 256 * x + 128 * t + 128] = tile
    width = 6 * 256
    place = lax.broadcasted_iota(jnp.int32, (16, width), 1)
    z = place % CZ
    y = (place % 256) // CZ
    whole = lines[...]
    for b in range(3):
        for c in range(3):
            step = CZ * (b - 1) + c - 1
            moved = pltpu.roll(whole, (-step) % width, 1) if step else whole
            keep = (z + (c - 1) >= 0) & (z + (c - 1) < CZ) & (y + (b - 1) >= 0) & (y + (b - 1) < 64)
            k = 3 * b + c
            shifted[16 * k : 16 * k + 16, :] = jnp.where(keep, moved, 0.0).astype(BF16)


def coarse_grad(shifted, field, out):
    chans = field.shape[2]
    cells = field[...].reshape(1024, chans)
    for a in range(3):
        term = dot(shifted[:, 256 * a : 256 * a + 1024], cells)
        for k in range(9):
            o = 26 - 9 * a - k
            for h in range(chans // 128):
                out[h, pl.ds(o, 16, stride=32), :] = term[16 * k : 16 * k + 16, 128 * h : 128 * h + 128]


def kernel(
    feat_hbm, cot_hbm, w_fine_hbm, w_down_hbm, w_mid_hbm,
    out_feat, out_fine, out_down, out_mid,
    feat, cot, own_c,
    w_fine, w_down, w_mid,
    ext_s, cols_s, border, border_s, turned_own, turned_s,
    ext_f, ext_c, ext_p, ext_d, ext_g,
    cols_f, cols_c, cols_p, cols_d, cols_g,
    own_p, own_d, own_g,
    sy_f, sc_f, rx_f, ry_f, rc_f,
    sy_c, sc_c, rx_c, ry_c, rc_c,
    sy_p, sc_p, rx_p, ry_p, rc_p,
    sy_d, sc_d, rx_d, ry_d, rc_d,
    sy_g, sc_g, rx_g, ry_g, rc_g,
    tmp, pairs, slope_f, delta_act, delta_pool, total_f,
    flip, lines, shifted_c, shifted_d, wide, spread,
    st_c, rt_c, st_d, rt_d, all_p, all_a,
    part, send_f, recv_f, fold_f,
    sx_m, rx_m, sx_d, rx_d2, sx_f, rx_f2,
    w_sem, s_send, s_recv, h_send, h_recv, a_send, a_recv,
):
    mx, my = lax.axis_index("gx"), lax.axis_index("gy")

    def other(axis, step):
        if axis == 0:
            return (lax.rem(mx + step, N), my)
        return (mx, lax.rem(my + step, N))

    barrier = pltpu.get_barrier_semaphore()

    def greet(d, carry):
        for axis in range(2):
            pl.semaphore_signal(barrier, inc=1, device_id=other(axis, d), device_id_type=MESH)
        return carry

    lax.fori_loop(1, N, greet, 0)
    for dx in (1, N - 1):
        for dy in (1, N - 1):
            there = (lax.rem(mx + dx, N), lax.rem(my + dy, N))
            pl.semaphore_signal(barrier, inc=1, device_id=there, device_id_type=MESH)

    loads = [
        pltpu.make_async_copy(src, dst, w_sem.at[i])
        for i, (src, dst) in enumerate(
            (
                (feat_hbm, feat),
                (cot_hbm, cot),
                (w_fine_hbm, w_fine),
                (w_mid_hbm, w_mid),
                (w_down_hbm, w_down),
            )
        )
    ]
    for load in loads:
        load.start()

    inside = ((mx > 0, mx < N - 1), (my > 0, my < N - 1))

    def neighbours(kind, first, last, send_y, send_c, recv_x, recv_y, recv_c):
        copies = []

        def add(src, dst, dx, dy):
            slot = len(copies)
            copies.append(
                pltpu.make_async_remote_copy(
                    src_ref=src,
                    dst_ref=dst,
                    send_sem=h_send.at[kind, slot],
                    recv_sem=h_recv.at[kind, slot],
                    device_id=(lax.rem(mx + dx + N, N), lax.rem(my + dy + N, N)),
                    device_id_type=MESH,
                )
            )

        add(first, recv_x.at[1], -1, 0)
        add(last, recv_x.at[0], 1, 0)
        for side in range(2):
            add(send_y.at[side], recv_y.at[1 - side], 0, 2 * side - 1)
        for end in range(2):
            for side in range(2):
                i = 2 * end + side
                add(send_c.at[i], recv_c.at[3 - i], 2 * end - 1, 2 * side - 1)
        return copies

    def exchange(kind, axis, src, dst):
        me = (mx, my)[axis]

        def copy(d, slot):
            return pltpu.make_async_remote_copy(
                src_ref=src(lax.rem(me + d, N)),
                dst_ref=dst(slot),
                send_sem=a_send.at[kind, d],
                recv_sem=a_recv.at[kind, d],
                device_id=other(axis, d),
                device_id_type=MESH,
            )

        def start():
            def body(d, carry):
                copy(d, me).start()
                return carry

            lax.fori_loop(1, N, body, 0)

        def arrive():
            def body(d, carry):
                copy(d, lax.rem(me - d + N, N)).wait_recv()
                return carry

            lax.fori_loop(1, N, body, 0)

        def leave():
            def body(d, carry):
                copy(d, me).wait_send()
                return carry

            lax.fori_loop(1, N, body, 0)

        return start, arrive, leave

    def sixteen(i):
        return pl.ds(pl.multiple_of(16 * i, 16), 16)

    halo_f = neighbours(FEAT, feat.at[0], feat.at[FX - 1], sy_f, sc_f, rx_f, ry_f, rc_f)
    halo_c = neighbours(COT, own_c.at[0], own_c.at[CX - 1], sy_c, sc_c, rx_c, ry_c, rc_c)
    halo_p = neighbours(POOL, own_p.at[0], own_p.at[CX - 1], sy_p, sc_p, rx_p, ry_p, rc_p)
    halo_d = neighbours(DC, own_d.at[0], own_d.at[CX - 1], sy_d, sc_d, rx_d, ry_d, rc_d)
    halo_g = neighbours(DF, own_g.at[0], own_g.at[FX - 1], sy_g, sc_g, rx_g, ry_g, rc_g)
    move_ct = exchange(COT_T, 1, lambda t: st_c.at[sixteen(t)], lambda s: rt_c.at[s])
    move_dt = exchange(DC_T, 1, lambda t: st_d.at[sixteen(t)], lambda s: rt_d.at[s])
    move_p = exchange(POOL_G, 1, lambda t: all_p.at[:, sixteen(my)], lambda s: all_p.at[:, sixteen(s)])
    move_a = exchange(ACT_G, 1, lambda t: all_a.at[:, sixteen(my)], lambda s: all_a.at[:, sixteen(s)])
    move_f = exchange(FINE, 1, lambda t: send_f.at[t], lambda s: recv_f.at[s])
    move_xm = exchange(X_MID, 0, lambda t: sx_m.at[t], lambda s: rx_m.at[s])
    move_xd = exchange(X_DOWN, 0, lambda t: sx_d.at[t], lambda s: rx_d2.at[s])
    move_xf = exchange(X_FINE, 0, lambda t: sx_f.at[t], lambda s: rx_f2.at[s])

    core = lax.rem(my, 2)
    sibling = (mx, my + 1 - 2 * core)

    def to_sibling(i, src, dst):
        return pltpu.make_async_remote_copy(
            src_ref=src,
            dst_ref=dst,
            send_sem=s_send.at[i],
            recv_sem=s_recv.at[i],
            device_id=sibling,
            device_id_type=MESH,
        )

    sib_feat = to_sibling(0, border, border_s)
    sib_delta = to_sibling(1, turned_own, turned_s)

    loads[0].wait()
    put_own(ext_f, feat[...].astype(F32), FZ)
    pack(ext_f, sy_f, sc_f, tmp, FZ)
    pl.semaphore_wait(barrier, 2 * (N - 1) + 4)
    for copy in halo_f:
        copy.start()
    loads[1].wait()
    lo, hi = own_rows(CZ)
    for x in range(CX):
        for y in range(CX):
            ext_c[1 + x, lo + CZ * y : lo + CZ * y + CZ, :] = cot[x, y].astype(F32)
    own_c[...] = ext_c[1 : CX + 1, lo:hi, :].astype(BF16)
    pack(ext_c, sy_c, sc_c, tmp, CZ)
    for copy in halo_c:
        copy.start()

    for copy in halo_f:
        copy.wait_recv()
    put_halo(ext_f, rx_f, ry_f, rc_f, inside, FZ)
    spread_lanes(ext_f, cols_f, FZ)
    loads[2].wait()
    pre = forward(cols_f, w_fine, FX)
    sig = jax.nn.sigmoid(pre)
    slope_f[...] = sig * (1.0 + pre * (1.0 - sig))
    act = (pre * sig).reshape(CX, 2, CX, 2, FZ, C3)
    pairs[...] = (act[:, 0, :, 0] + act[:, 0, :, 1] + act[:, 1, :, 0] + act[:, 1, :, 1]).reshape(128, C3)
    pooled = (pairs[pl.ds(0, 64, stride=2), :] + pairs[pl.ds(1, 64, stride=2), :]) * 0.125
    pooled = pooled.astype(BF16).reshape(CX, CR, C3)
    own_p[...] = pooled
    put_own(ext_p, pooled.astype(F32), CZ)
    pack(ext_p, sy_p, sc_p, tmp, CZ)
    for copy in halo_p:
        copy.start()
    border[...] = ext_f[:, BASE : BASE + FZ * (FX + 2), :].astype(BF16)
    sib_feat.start()
    all_p[:, sixteen(my), :] = pooled
    move_p[0]()

    for copy in halo_c:
        copy.wait_recv()
    put_halo(ext_c, rx_c, ry_c, rc_c, inside, CZ)
    send_chunks(ext_c, flip, st_c)
    move_ct[0]()
    rt_c[my] = st_c[sixteen(my), :]
    spread_lanes(ext_c, cols_c, CZ)
    loads[3].wait()
    backward(cols_c, w_mid, CX, delta_act)

    for copy in halo_p:
        copy.wait_recv()
    put_halo(ext_p, rx_p, ry_p, rc_p, inside, CZ)
    spread_lanes(ext_p, cols_p, CZ)
    loads[4].wait()
    pre = forward(cols_p, w_down, CX)
    sig = jax.nn.sigmoid(pre)
    delta = (delta_act[...] * (sig * (1.0 + pre * (1.0 - sig)))).astype(BF16).reshape(CX, CR, C4)
    own_d[...] = delta
    put_own(ext_d, delta.astype(F32), CZ)
    pack(ext_d, sy_d, sc_d, tmp, CZ)
    for copy in halo_d:
        copy.start()
    all_a[:, sixteen(my), :] = (pre * sig).astype(BF16).reshape(CX, CR, C4)
    move_a[0]()
    sib_feat.wait_recv()
    ext_s[:, BASE : BASE + FZ * (FX + 2), :] = border_s[...].astype(F32)
    spread_lanes(ext_s, cols_s, FZ)
    move_ct[1]()
    gather_lanes(rt_c, lines, shifted_c)

    for copy in halo_d:
        copy.wait_recv()
    put_halo(ext_d, rx_d, ry_d, rc_d, inside, CZ)
    spread_lanes(ext_d, cols_d, CZ)
    backward(cols_d, w_down, CX, delta_pool)
    pooled_delta = delta_pool[...] * 0.125
    pairs[pl.ds(0, 64, stride=2), :] = pooled_delta
    pairs[pl.ds(1, 64, stride=2), :] = pooled_delta
    up = jnp.broadcast_to(pairs[...].reshape(CX, 1, CX, 1, FZ, C3), (CX, 2, CX, 2, FZ, C3))
    delta = (up.reshape(512, C3) * slope_f[...]).astype(BF16)
    turned_own[...] = delta.astype(F32).T.astype(BF16)
    sib_delta.start()
    send_chunks(ext_d, flip, st_d)
    move_dt[0]()
    rt_d[my] = st_d[sixteen(my), :]

    lanes = pl.ds(pl.multiple_of(4 * C3 * core, C3), 5 * C3)

    def half(turned, cols):
        part[:, 0 : 9 * C3] += dot(turned, cols[pl.ds(2 * core, FX)].reshape(512, 9 * C3))
        part[:, 9 * C3 : 14 * C3] += dot(turned, cols[1 : 1 + FX, :, lanes].reshape(512, 5 * C3))

    part[...] = jnp.zeros(part.shape, F32)
    half(turned_own[...], cols_f)
    sib_delta.wait_recv()
    half(turned_s[...], cols_s)

    def fold(j, carry):
        rows = pl.ds(pl.multiple_of(8 * j, 8), 8)
        send_f[j] = jnp.concatenate([part[rows, 0:HALF], part[rows, HALF : 2 * HALF]], axis=0).astype(BF16)
        return carry

    lax.fori_loop(0, N, fold, 0)
    move_f[0]()
    recv_f[my] = send_f[my]
    own_g[...] = delta.reshape(FX, FR, C3)
    put_own(ext_g, delta.astype(F32).reshape(FX, FR, C3), FZ)
    pack(ext_g, sy_g, sc_g, tmp, FZ)
    for copy in halo_g:
        copy.start()

    move_a[1]()
    coarse_grad(shifted_c, all_a, wide)
    for h in range(2):
        sx_m[8 * h : 8 * h + 8] = wide[h].T.astype(BF16).reshape(8, 16, 512)
    move_xm[0]()
    rx_m[mx] = sx_m[mx]

    move_dt[1]()
    gather_lanes(rt_d, lines, shifted_d)
    move_p[1]()
    coarse_grad(shifted_d, all_p, wide)
    turned = wide[0].T
    for i in range(N):
        rows = turned[8 * i : 8 * i + 8]
        sx_d[i] = jnp.concatenate([rows[:, 0:256], rows[:, 256:512]], axis=0).astype(BF16)
    move_xd[0]()
    rx_d2[mx] = sx_d[mx]

    for copy in halo_g:
        copy.wait_recv()
    put_halo(ext_g, rx_g, ry_g, rc_g, inside, FZ)
    spread_lanes(ext_g, cols_g, FZ)
    backward(cols_g, w_fine, FX, total_f)
    out_feat[...] = total_f[...].astype(BF16).reshape(FX, FR, C3)

    move_f[1]()

    def add_f(s, totals):
        return tuple(totals[c] + recv_f[2 * s + c].astype(F32) for c in range(2))

    nothing = jnp.zeros((16, HALF), F32)
    totals = lax.fori_loop(0, N // 2, add_f, (nothing, nothing))
    for o in range(27):
        c, i = (0, o) if o < 14 else (1, o - 18 if o >= 18 else o - 4)
        half_at, at = divmod(i, 7)
        fold_f[pl.ds(o, 8, stride=32), :] = totals[c][8 * half_at : 8 * half_at + 8, C3 * at : C3 * at + C3]
    turned = fold_f[...].T
    for i in range(N):
        rows = turned[8 * i : 8 * i + 8]
        sx_f[i] = jnp.concatenate([rows[:, 0:128], rows[:, 128:256]], axis=0).astype(BF16)
    move_xf[0]()
    rx_f2[mx] = sx_f[mx]

    def summed(arrived):
        def add(s, total):
            return total + arrived[s].astype(F32)

        return lax.fori_loop(0, N, add, jnp.zeros(arrived.shape[1:], F32))

    def unfold(out, total, rows, first, most):
        for co in range(first, first + most):
            at = 32 * (co - first)
            spread[pl.ds(co, rows, stride=out.shape[0] // rows), 0:32] = total[:, at : at + 32]
        out[...] = spread[0 : out.shape[0], 0:27]

    coarse_scale = 1.0 / math.sqrt(CX * N * CX * N * CZ)
    move_xm[1]()
    unfold(out_mid, summed(rx_m) * coarse_scale, 16, 0, 16)
    move_xd[1]()
    total = summed(rx_d2) * coarse_scale
    unfold(out_down, total[0:8], 8, 0, 8)
    unfold(out_down, total[8:16], 8, 8, 8)
    move_xf[1]()
    total = summed(rx_f2) * (1.0 / math.sqrt(FX * N * FX * N * FZ))
    unfold(out_fine, total[0:8], 8, 0, 4)
    unfold(out_fine, total[8:16], 8, 4, 4)

    for copy in halo_f + halo_c + halo_p + halo_d + halo_g + [sib_feat, sib_delta]:
        copy.wait_send()
    for move in (move_ct, move_dt, move_p, move_a, move_f, move_xm, move_xd, move_xf):
        move[2]()


def halo_scratch(nx, rows, chans):
    lines = nx * rows // nx
    return [
        pltpu.VMEM((2, lines, chans), BF16),
        pltpu.VMEM((4, 16, chans), BF16),
        pltpu.VMEM((2, rows, chans), BF16),
        pltpu.VMEM((2, lines, chans), BF16),
        pltpu.VMEM((4, 16, chans), BF16),
    ]


def hand_over(*refs):
    for i in range(4):
        refs[4 + i][...] = refs[i][...]


def per_device(features, weight_fine, weight_down, weight_mid, cotangent):
    vmem = pl.BlockSpec(memory_space=pltpu.VMEM)
    hbm = pl.BlockSpec(memory_space=pltpu.HBM)
    fine_ext = pltpu.VMEM((FX + 2, 2 * BASE + FZ * (FX + 2), C3), F32)
    fine_cols = pltpu.VMEM((FX + 2, FR, 9 * C3), BF16)

    def coarse_ext(chans):
        return pltpu.VMEM((CX + 2, 2 * BASE + CZ * (CX + 2), chans), F32)

    def coarse_cols(chans):
        return pltpu.VMEM((CX + 2, CR, 9 * chans), BF16)

    scratch = [
        pltpu.VMEM((FX, FR, C3), BF16),
        pltpu.VMEM((CX, CX, CZ, C4), BF16),
        pltpu.VMEM((CX, CR, C4), BF16),
        pltpu.VMEM((27, C3, C3), BF16),
        pltpu.VMEM((27, C3, C4), BF16),
        pltpu.VMEM((27, C4, C4), BF16),
        fine_ext, fine_cols,
        pltpu.VMEM((FX + 2, FZ * (FX + 2), C3), BF16),
        pltpu.VMEM((FX + 2, FZ * (FX + 2), C3), BF16),
        pltpu.VMEM((C3, 512), BF16),
        pltpu.VMEM((C3, 512), BF16),
        fine_ext, coarse_ext(C4), coarse_ext(C3), coarse_ext(C4), fine_ext,
        fine_cols, coarse_cols(C4), coarse_cols(C3), coarse_cols(C4), fine_cols,
        pltpu.VMEM((CX, CR, C3), BF16),
        pltpu.VMEM((CX, CR, C4), BF16),
        pltpu.VMEM((FX, FR, C3), BF16),
        *halo_scratch(FX, FR, C3),
        *halo_scratch(CX, CR, C4),
        *halo_scratch(CX, CR, C3),
        *halo_scratch(CX, CR, C4),
        *halo_scratch(FX, FR, C3),
        pltpu.VMEM((2, 16, C4), F32),
        pltpu.VMEM((128, C3), F32),
        pltpu.VMEM((512, C3), F32),
        pltpu.VMEM((64, C4), F32),
        pltpu.VMEM((64, C3), F32),
        pltpu.VMEM((512, C3), F32),
        pltpu.VMEM((128, C4), F32),
        pltpu.VMEM((16, 6 * 256), F32),
        pltpu.VMEM((144, 6 * 256), BF16),
        pltpu.VMEM((144, 6 * 256), BF16),
        pltpu.VMEM((2, 512, 128), F32),
        pltpu.VMEM((16 * 16, 128), F32),
        pltpu.VMEM((C4, 128), BF16),
        pltpu.VMEM((N, 16, 128), BF16),
        pltpu.VMEM((C4, 128), BF16),
        pltpu.VMEM((N, 16, 128), BF16),
        pltpu.VMEM((CX, N * CR, C3), BF16),
        pltpu.VMEM((CX, N * CR, C4), BF16),
        pltpu.VMEM((C3, 2 * HALF), F32),
        pltpu.VMEM((N, 16, HALF), BF16),
        pltpu.VMEM((N, 16, HALF), BF16),
        pltpu.VMEM((256, C3), F32),
        pltpu.VMEM((N, 16, 512), BF16),
        pltpu.VMEM((N, 16, 512), BF16),
        pltpu.VMEM((N, 16, 256), BF16),
        pltpu.VMEM((N, 16, 256), BF16),
        pltpu.VMEM((N, 16, 128), BF16),
        pltpu.VMEM((N, 16, 128), BF16),
        pltpu.SemaphoreType.DMA((5,)),
        pltpu.SemaphoreType.DMA((2,)),
        pltpu.SemaphoreType.DMA((2,)),
        pltpu.SemaphoreType.DMA((5, 8)),
        pltpu.SemaphoreType.DMA((5, 8)),
        pltpu.SemaphoreType.DMA((8, N)),
        pltpu.SemaphoreType.DMA((8, N)),
    ]
    shapes = (
            jax.ShapeDtypeStruct((FX, FR, C3), BF16),
            jax.ShapeDtypeStruct((8 * 8, 27), F32),
            jax.ShapeDtypeStruct((8 * 16, 27), F32),
            jax.ShapeDtypeStruct((16 * 16, 27), F32),
    )
    results = pl.pallas_call(
        kernel,
        out_shape=shapes,
        in_specs=[hbm] * 5,
        out_specs=(vmem, vmem, vmem, vmem),
        scratch_shapes=scratch,
        compiler_params=pltpu.CompilerParams(
            collective_id=0, has_side_effects=True, vmem_limit_bytes=61 * 1024 * 1024
        ),
        name="unet_backward",
    )(
        features.reshape(FX, FR, C3),
        cotangent,
        weight_fine,
        weight_down,
        weight_mid,
    )
    out_feat, out_fine, out_down, out_mid = pl.pallas_call(
        hand_over,
        out_shape=shapes,
        in_specs=[vmem] * 4,
        out_specs=(vmem,) * 4,
        name="hand_over",
    )(*results)
    return (
        out_feat.reshape(FX, FX, FZ, C3),
        out_fine.reshape(8, 8, 27).transpose(0, 2, 1),
        out_down.reshape(8, 16, 27).transpose(0, 2, 1),
        out_mid.reshape(16, 16, 27).transpose(0, 2, 1),
    )


def solution(mesh):
    in_specs = (P("gx", "gy", None, None), P(), P(), P(), P("gx", "gy", None, None))
    out_specs = (
        P("gx", "gy", None, None),
        P("gx", None, "gy"),
        P("gx", None, "gy"),
        P("gx", None, "gy"),
    )
    return jax.shard_map(
        per_device, mesh=mesh, in_specs=in_specs, out_specs=out_specs, check_vma=False
    )
```

```python
import math

import jax
import jax.numpy as jnp
from jax import lax
from jax.experimental import pallas as pl
from jax.experimental.pallas import tpu as pltpu
from jax.sharding import PartitionSpec as P

MESH = pl.DeviceIdType.MESH
F32 = jnp.float32
BF16 = jnp.bfloat16

N = 16
BASE = 8
FX, FZ, C3 = 8, 8, 128
CX, CZ, C4 = 4, 4, 256
FR, CR = FX * FZ, CX * CZ
HALF = 7 * C3

FEAT, COT, POOL, DF = range(4)
COT_T, POOL_G, ACT_G, DC_T, FINE, X_MID, X_DOWN, X_FINE = range(8)


def dot(a, b):
    return jnp.dot(a, b, preferred_element_type=F32)


def dot_t(a, b):
    return lax.dot_general(a, b, (((1,), (1,)), ((), ())), preferred_element_type=F32)


def kept(flag, value):
    return jnp.where(flag, value.astype(F32), 0.0)


def frame(reach):
    nx, nz = (FX, FZ) if reach == 1 else (CX, CZ)
    lo = BASE + 8
    return nx, lo, lo + nx * nz


def put_own(ext, own, reach):
    nx, lo, hi = frame(reach)
    ext[reach : reach + nx, lo:hi, :] = own


def pack(ext, send_y, send_c, reach):
    nx, lo, hi = frame(reach)
    chans = ext.shape[2]
    for side, start in ((0, lo), (1, hi - 8)):
        send_y[side] = ext[reach : reach + nx, start : start + 8, :].reshape(nx * 8, chans).astype(BF16)
        for end, x in ((0, reach), (1, nx)):
            if reach == 1:
                send_c[2 * end + side] = ext[x, start : start + 16, :].astype(BF16)
            else:
                send_c[2 * end + side] = ext[x : x + 2, start : start + 8, :].reshape(16, chans).astype(BF16)


def put_halo(ext, recv_x, recv_y, recv_c, inside, reach):
    nx, lo, hi = frame(reach)
    chans = ext.shape[2]
    for end, x in ((0, 0), (1, reach + nx)):
        ext[x : x + reach, lo:hi, :] = kept(inside[0][end], recv_x[end]).reshape(reach, hi - lo, chans)
    for side, start in ((0, lo - 8), (1, hi)):
        line = kept(inside[1][side], recv_y[side])
        ext[reach : reach + nx, start : start + 8, :] = line.reshape(nx, 8, chans)
        for end, x in ((0, 0), (1, reach + nx)):
            flag = jnp.logical_and(inside[0][end], inside[1][side])
            corner = kept(flag, recv_c[2 * end + side])[0 : 8 * reach]
            ext[x : x + reach, start : start + 8, :] = corner.reshape(reach, 8, chans)


def spread_lanes(ext, cols, nz):
    lo = BASE + nz
    rows = cols.shape[1]
    chans = ext.shape[2]
    z = lax.broadcasted_iota(jnp.int32, (rows, chans), 0) % nz

    def layer(x, carry):
        for b in range(3):
            for c in range(3):
                piece = ext[x, pl.ds(lo + nz * (b - 1) + c - 1, rows), :]
                if c == 0:
                    piece = jnp.where(z >= 1, piece, 0.0)
                if c == 2:
                    piece = jnp.where(z <= nz - 2, piece, 0.0)
                k = 3 * b + c
                cols[x, :, k * chans : (k + 1) * chans] = piece.astype(BF16)
        return carry

    lax.fori_loop(0, ext.shape[0], layer, 0)


def forward(cols, weight, nx):
    rows, depth = cols.shape[1], cols.shape[2]
    total = None
    for a in range(3):
        term = dot(
            cols[a : a + nx].reshape(nx * rows, depth),
            weight[9 * a : 9 * a + 9].reshape(depth, weight.shape[2]),
        )
        total = term if total is None else total + term
    return total


def backward(cols, weight, nx, total):
    rows = cols.shape[1]
    chans = weight.shape[2]
    for a in range(3):
        for k in range(9):
            piece = cols[a : a + nx, :, k * chans : (k + 1) * chans].reshape(nx * rows, chans)
            term = dot_t(piece, weight[26 - 9 * a - k])
            if a == 0 and k == 0:
                total[...] = term
            else:
                total[...] += term


def send_chunks(layers, flip, send_t):
    flip[0:96, :] = layers.reshape(96, C4)
    send_t[...] = flip[...].T.astype(BF16)


def gather_lanes(recv_t, lines, shifted):
    lane = lax.broadcasted_iota(jnp.int32, (16, 128), 1) // 16
    for t in range(2):
        pieces = [recv_t[8 * t + s].astype(F32) for s in range(8)]
        for x in range(6):
            tile = jnp.zeros((16, 128), F32)
            for s in range(8):
                moved = pltpu.roll(pieces[s], (16 * s - 16 * x) % 128, 1) if s != x else pieces[s]
                tile = jnp.where(lane == s, moved, tile)
            lines[:, 256 * x + 128 * t : 256 * x + 128 * t + 128] = tile
    width = 6 * 256
    place = lax.broadcasted_iota(jnp.int32, (16, width), 1)
    z = place % CZ
    y = (place % 256) // CZ
    whole = lines[...]
    for b in range(3):
        for c in range(3):
            step = CZ * (b - 1) + c - 1
            moved = pltpu.roll(whole, (-step) % width, 1) if step else whole
            keep = (z + (c - 1) >= 0) & (z + (c - 1) < CZ) & (y + (b - 1) >= 0) & (y + (b - 1) < 64)
            k = 3 * b + c
            shifted[16 * k : 16 * k + 16, :] = jnp.where(keep, moved, 0.0).astype(BF16)


def coarse_grad(shifted, field, out):
    chans = field.shape[2]
    cells = field[...].reshape(1024, chans)
    for a in range(3):
        term = dot(shifted[:, 256 * a : 256 * a + 1024], cells)
        for k in range(9):
            o = 26 - 9 * a - k
            for h in range(chans // 128):
                out[h, pl.ds(o, 16, stride=32), :] = term[16 * k : 16 * k + 16, 128 * h : 128 * h + 128]


def kernel(
    feat_hbm, cot_hbm, w_fine_hbm, w_down_hbm, w_mid_hbm,
    out_feat, out_fine, out_down, out_mid,
    feat, cot, own_c,
    w_fine, w_down, w_mid,
    ext_s, cols_s, border, border_s, turned_own, turned_s,
    ext_f, ext_c, ext_p, ext_d, ext_g,
    cols_f, cols_c, cols_p, cols_d, cols_g,
    own_p, own_g,
    sy_f, sc_f, rx_f, ry_f, rc_f,
    sy_c, sc_c, rx_c, ry_c, rc_c,
    sy_p, sc_p, rx_p, ry_p, rc_p,
    sy_g, sc_g, rx_g, ry_g, rc_g,
    act_c, pairs, slope_f, delta_act, delta_pool, total_f,
    flip, lines, shifted_c, shifted_d, wide, spread,
    st_c, rt_c, st_d, rt_d, all_p, all_a,
    part, send_f, recv_f, fold_f,
    sx_m, rx_m, sx_d, rx_d2, sx_f, rx_f2,
    w_sem, s_send, s_recv, h_send, h_recv, a_send, a_recv,
):
    mx, my = lax.axis_index("gx"), lax.axis_index("gy")

    def other(axis, step):
        if axis == 0:
            return (lax.rem(mx + step, N), my)
        return (mx, lax.rem(my + step, N))

    barrier = pltpu.get_barrier_semaphore()

    def greet(d, carry):
        for axis in range(2):
            pl.semaphore_signal(barrier, inc=1, device_id=other(axis, d), device_id_type=MESH)
        return carry

    lax.fori_loop(1, N, greet, 0)
    for dx in (1, N - 1):
        for dy in (1, N - 1):
            there = (lax.rem(mx + dx, N), lax.rem(my + dy, N))
            pl.semaphore_signal(barrier, inc=1, device_id=there, device_id_type=MESH)

    loads = [
        pltpu.make_async_copy(src, dst, w_sem.at[i])
        for i, (src, dst) in enumerate(
            (
                (feat_hbm, feat),
                (cot_hbm, cot),
                (w_fine_hbm, w_fine),
                (w_mid_hbm, w_mid),
                (w_down_hbm, w_down),
            )
        )
    ]
    for load in loads:
        load.start()

    inside = ((mx > 0, mx < N - 1), (my > 0, my < N - 1))

    def neighbours(kind, first, last, send_y, send_c, recv_x, recv_y, recv_c):
        copies = []

        def add(src, dst, dx, dy):
            slot = len(copies)
            copies.append(
                pltpu.make_async_remote_copy(
                    src_ref=src,
                    dst_ref=dst,
                    send_sem=h_send.at[kind, slot],
                    recv_sem=h_recv.at[kind, slot],
                    device_id=(lax.rem(mx + dx + N, N), lax.rem(my + dy + N, N)),
                    device_id_type=MESH,
                )
            )

        add(first, recv_x.at[1], -1, 0)
        add(last, recv_x.at[0], 1, 0)
        for side in range(2):
            add(send_y.at[side], recv_y.at[1 - side], 0, 2 * side - 1)
        for end in range(2):
            for side in range(2):
                i = 2 * end + side
                add(send_c.at[i], recv_c.at[3 - i], 2 * end - 1, 2 * side - 1)
        return copies

    def exchange(kind, axis, src, dst):
        me = (mx, my)[axis]

        def copy(d, slot):
            return pltpu.make_async_remote_copy(
                src_ref=src(lax.rem(me + d, N)),
                dst_ref=dst(slot),
                send_sem=a_send.at[kind, d],
                recv_sem=a_recv.at[kind, d],
                device_id=other(axis, d),
                device_id_type=MESH,
            )

        def start():
            def body(d, carry):
                copy(d, me).start()
                return carry

            lax.fori_loop(1, N, body, 0)

        def arrive():
            def body(d, carry):
                copy(d, lax.rem(me - d + N, N)).wait_recv()
                return carry

            lax.fori_loop(1, N, body, 0)

        def leave():
            def body(d, carry):
                copy(d, me).wait_send()
                return carry

            lax.fori_loop(1, N, body, 0)

        return start, arrive, leave

    def sixteen(i):
        return pl.ds(pl.multiple_of(16 * i, 16), 16)

    halo_f = neighbours(FEAT, feat.at[0], feat.at[FX - 1], sy_f, sc_f, rx_f, ry_f, rc_f)
    halo_c = neighbours(COT, own_c.at[0:2], own_c.at[CX - 2 : CX], sy_c, sc_c, rx_c, ry_c, rc_c)
    halo_p = neighbours(POOL, own_p.at[0:2], own_p.at[CX - 2 : CX], sy_p, sc_p, rx_p, ry_p, rc_p)
    halo_g = neighbours(DF, own_g.at[0], own_g.at[FX - 1], sy_g, sc_g, rx_g, ry_g, rc_g)
    move_ct = exchange(COT_T, 1, lambda t: st_c.at[sixteen(t)], lambda s: rt_c.at[s])
    move_dt = exchange(DC_T, 1, lambda t: st_d.at[sixteen(t)], lambda s: rt_d.at[s])
    move_p = exchange(POOL_G, 1, lambda t: all_p.at[:, sixteen(my)], lambda s: all_p.at[:, sixteen(s)])
    move_a = exchange(ACT_G, 1, lambda t: all_a.at[:, sixteen(my)], lambda s: all_a.at[:, sixteen(s)])
    move_f = exchange(FINE, 1, lambda t: send_f.at[t], lambda s: recv_f.at[s])
    move_xm = exchange(X_MID, 0, lambda t: sx_m.at[t], lambda s: rx_m.at[s])
    move_xd = exchange(X_DOWN, 0, lambda t: sx_d.at[t], lambda s: rx_d2.at[s])
    move_xf = exchange(X_FINE, 0, lambda t: sx_f.at[t], lambda s: rx_f2.at[s])

    core = lax.rem(my, 2)
    sibling = (mx, my + 1 - 2 * core)

    def to_sibling(i, src, dst):
        return pltpu.make_async_remote_copy(
            src_ref=src,
            dst_ref=dst,
            send_sem=s_send.at[i],
            recv_sem=s_recv.at[i],
            device_id=sibling,
            device_id_type=MESH,
        )

    sib_feat = to_sibling(0, border, border_s)
    sib_delta = to_sibling(1, turned_own, turned_s)

    loads[0].wait()
    put_own(ext_f, feat[...].astype(F32), 1)
    pack(ext_f, sy_f, sc_f, 1)
    pl.semaphore_wait(barrier, 2 * (N - 1) + 4)
    for copy in halo_f:
        copy.start()
    loads[1].wait()
    nx, lo, hi = frame(2)
    for x in range(CX):
        for y in range(CX):
            ext_c[2 + x, lo + CZ * y : lo + CZ * y + CZ, :] = cot[x, y].astype(F32)
    own_c[...] = ext_c[2 : CX + 2, lo:hi, :].astype(BF16)
    pack(ext_c, sy_c, sc_c, 2)
    for copy in halo_c:
        copy.start()

    for copy in halo_f:
        copy.wait_recv()
    put_halo(ext_f, rx_f, ry_f, rc_f, inside, 1)
    spread_lanes(ext_f, cols_f, FZ)
    loads[2].wait()
    pre = forward(cols_f, w_fine, FX)
    sig = jax.nn.sigmoid(pre)
    slope_f[...] = sig * (1.0 + pre * (1.0 - sig))
    act = (pre * sig).reshape(CX, 2, CX, 2, FZ, C3)
    pairs[...] = (act[:, 0, :, 0] + act[:, 0, :, 1] + act[:, 1, :, 0] + act[:, 1, :, 1]).reshape(128, C3)
    pooled = (pairs[pl.ds(0, 64, stride=2), :] + pairs[pl.ds(1, 64, stride=2), :]) * 0.125
    pooled = pooled.astype(BF16).reshape(CX, CR, C3)
    own_p[...] = pooled
    put_own(ext_p, pooled.astype(F32), 2)
    pack(ext_p, sy_p, sc_p, 2)
    for copy in halo_p:
        copy.start()
    border[...] = ext_f[:, BASE : BASE + FZ * (FX + 2), :].astype(BF16)
    sib_feat.start()
    all_p[:, sixteen(my), :] = pooled
    move_p[0]()

    for copy in halo_c:
        copy.wait_recv()
    put_halo(ext_c, rx_c, ry_c, rc_c, inside, 2)
    send_chunks(ext_c[1:7, lo:hi, :], flip, st_c)
    move_ct[0]()
    rt_c[my] = st_c[sixteen(my), :]
    spread_lanes(ext_c, cols_c, CZ)
    loads[3].wait()
    backward(cols_c, w_mid, CX + 2, delta_act)
    sib_feat.wait_recv()
    ext_s[:, BASE : BASE + FZ * (FX + 2), :] = border_s[...].astype(F32)
    spread_lanes(ext_s, cols_s, FZ)

    for copy in halo_p:
        copy.wait_recv()
    put_halo(ext_p, rx_p, ry_p, rc_p, inside, 2)
    spread_lanes(ext_p, cols_p, CZ)
    loads[4].wait()
    pre = forward(cols_p, w_down, CX + 2)
    sig = jax.nn.sigmoid(pre)
    act_c[...] = (pre * sig).reshape(CX + 2, 32, C4)
    all_a[:, sixteen(my), :] = act_c[1 : CX + 1, CZ : CZ + CR, :].astype(BF16)
    move_a[0]()
    delta = (delta_act[...] * (sig * (1.0 + pre * (1.0 - sig)))).astype(BF16).astype(F32)
    last = BASE + CZ * (CX + 2)
    ext_d[:, BASE:last, :] = delta.reshape(CX + 2, 32, C4)[:, 0 : CZ * (CX + 2), :]
    for end, x in ((0, 0), (1, CX + 1)):
        ext_d[x, BASE:last, :] = kept(inside[0][end], ext_d[x, BASE:last, :])
    for side, start in ((0, BASE), (1, last - CZ)):
        ext_d[:, start : start + CZ, :] = kept(inside[1][side], ext_d[:, start : start + CZ, :])

    spread_lanes(ext_d, cols_d, CZ)
    backward(cols_d, w_down, CX, delta_pool)
    pooled_delta = delta_pool[...] * 0.125
    pairs[pl.ds(0, 64, stride=2), :] = pooled_delta
    pairs[pl.ds(1, 64, stride=2), :] = pooled_delta
    up = jnp.broadcast_to(pairs[...].reshape(CX, 1, CX, 1, FZ, C3), (CX, 2, CX, 2, FZ, C3))
    delta = (up.reshape(512, C3) * slope_f[...]).astype(BF16)
    turned_own[...] = delta.astype(F32).T.astype(BF16)
    sib_delta.start()
    send_chunks(ext_d[:, 12:28, :], flip, st_d)
    move_dt[0]()
    rt_d[my] = st_d[sixteen(my), :]

    lanes = pl.ds(pl.multiple_of(4 * C3 * core, C3), 5 * C3)

    def half(turned, cols):
        part[:, 0 : 9 * C3] += dot(turned, cols[pl.ds(2 * core, FX)].reshape(512, 9 * C3))
        part[:, 9 * C3 : 14 * C3] += dot(turned, cols[1 : 1 + FX, :, lanes].reshape(512, 5 * C3))

    part[...] = jnp.zeros(part.shape, F32)
    half(turned_own[...], cols_f)
    move_ct[1]()
    gather_lanes(rt_c, lines, shifted_c)

    sib_delta.wait_recv()
    half(turned_s[...], cols_s)

    def fold(j, carry):
        rows = pl.ds(pl.multiple_of(8 * j, 8), 8)
        send_f[j] = jnp.concatenate([part[rows, 0:HALF], part[rows, HALF : 2 * HALF]], axis=0).astype(BF16)
        return carry

    lax.fori_loop(0, N, fold, 0)
    move_f[0]()
    recv_f[my] = send_f[my]
    own_g[...] = delta.reshape(FX, FR, C3)
    put_own(ext_g, delta.astype(F32).reshape(FX, FR, C3), 1)
    pack(ext_g, sy_g, sc_g, 1)
    for copy in halo_g:
        copy.start()

    move_a[1]()
    coarse_grad(shifted_c, all_a, wide)
    for h in range(2):
        sx_m[8 * h : 8 * h + 8] = wide[h].T.astype(BF16).reshape(8, 16, 512)
    move_xm[0]()
    rx_m[mx] = sx_m[mx]

    move_dt[1]()
    gather_lanes(rt_d, lines, shifted_d)
    move_p[1]()
    coarse_grad(shifted_d, all_p, wide)
    turned = wide[0].T
    for i in range(N):
        rows = turned[8 * i : 8 * i + 8]
        sx_d[i] = jnp.concatenate([rows[:, 0:256], rows[:, 256:512]], axis=0).astype(BF16)
    move_xd[0]()
    rx_d2[mx] = sx_d[mx]

    move_f[1]()

    def add_f(s, totals):
        return tuple(totals[c] + recv_f[2 * s + c].astype(F32) for c in range(2))

    nothing = jnp.zeros((16, HALF), F32)
    totals = lax.fori_loop(0, N // 2, add_f, (nothing, nothing))
    for o in range(27):
        c, i = (0, o) if o < 14 else (1, o - 18 if o >= 18 else o - 4)
        half_at, at = divmod(i, 7)
        fold_f[pl.ds(o, 8, stride=32), :] = totals[c][8 * half_at : 8 * half_at + 8, C3 * at : C3 * at + C3]
    turned = fold_f[...].T
    for i in range(N):
        rows = turned[8 * i : 8 * i + 8]
        sx_f[i] = jnp.concatenate([rows[:, 0:128], rows[:, 128:256]], axis=0).astype(BF16)
    move_xf[0]()
    rx_f2[mx] = sx_f[mx]

    for copy in halo_g:
        copy.wait_recv()
    put_halo(ext_g, rx_g, ry_g, rc_g, inside, 1)
    spread_lanes(ext_g, cols_g, FZ)
    backward(cols_g, w_fine, FX, total_f)
    out_feat[...] = total_f[...].astype(BF16).reshape(FX, FR, C3)

    def summed(arrived):
        def add(s, total):
            return total + arrived[s].astype(F32)

        return lax.fori_loop(0, N, add, jnp.zeros(arrived.shape[1:], F32))

    def unfold(out, total, rows, first, most):
        for co in range(first, first + most):
            at = 32 * (co - first)
            spread[pl.ds(co, rows, stride=out.shape[0] // rows), 0:32] = total[:, at : at + 32]
        out[...] = spread[0 : out.shape[0], 0:27]

    coarse_scale = 1.0 / math.sqrt(CX * N * CX * N * CZ)
    move_xm[1]()
    unfold(out_mid, summed(rx_m) * coarse_scale, 16, 0, 16)
    move_xd[1]()
    total = summed(rx_d2) * coarse_scale
    unfold(out_down, total[0:8], 8, 0, 8)
    unfold(out_down, total[8:16], 8, 8, 8)
    move_xf[1]()
    total = summed(rx_f2) * (1.0 / math.sqrt(FX * N * FX * N * FZ))
    unfold(out_fine, total[0:8], 8, 0, 4)
    unfold(out_fine, total[8:16], 8, 4, 4)

    for copy in halo_f + halo_c + halo_p + halo_g + [sib_feat, sib_delta]:
        copy.wait_send()
    for move in (move_ct, move_dt, move_p, move_a, move_f, move_xm, move_xd, move_xf):
        move[2]()


def halo_scratch(lines, layers):
    chans = layers[-1]
    return [
        pltpu.VMEM((2, lines, chans), BF16),
        pltpu.VMEM((4, 16, chans), BF16),
        pltpu.VMEM((2, *layers), BF16),
        pltpu.VMEM((2, lines, chans), BF16),
        pltpu.VMEM((4, 16, chans), BF16),
    ]


def hand_over(*refs):
    for i in range(4):
        refs[4 + i][...] = refs[i][...]


def per_device(features, weight_fine, weight_down, weight_mid, cotangent):
    vmem = pl.BlockSpec(memory_space=pltpu.VMEM)
    hbm = pl.BlockSpec(memory_space=pltpu.HBM)
    fine_ext = pltpu.VMEM((FX + 2, 2 * BASE + FZ * (FX + 2), C3), F32)
    fine_cols = pltpu.VMEM((FX + 2, FR, 9 * C3), BF16)

    def wide_ext(chans):
        return pltpu.VMEM((CX + 4, 3 * BASE + CZ * (CX + 4), chans), F32)

    def wide_cols(chans):
        return pltpu.VMEM((CX + 4, 32, 9 * chans), BF16)

    ext_d = pltpu.VMEM((CX + 2, 2 * BASE + CZ * (CX + 2), C4), F32)
    cols_d = pltpu.VMEM((CX + 2, CR, 9 * C4), BF16)

    scratch = [
        pltpu.VMEM((FX, FR, C3), BF16),
        pltpu.VMEM((CX, CX, CZ, C4), BF16),
        pltpu.VMEM((CX, CR, C4), BF16),
        pltpu.VMEM((27, C3, C3), BF16),
        pltpu.VMEM((27, C3, C4), BF16),
        pltpu.VMEM((27, C4, C4), BF16),
        fine_ext, fine_cols,
        pltpu.VMEM((FX + 2, FZ * (FX + 2), C3), BF16),
        pltpu.VMEM((FX + 2, FZ * (FX + 2), C3), BF16),
        pltpu.VMEM((C3, 512), BF16),
        pltpu.VMEM((C3, 512), BF16),
        fine_ext, wide_ext(C4), wide_ext(C3), ext_d, fine_ext,
        fine_cols, wide_cols(C4), wide_cols(C3), cols_d, fine_cols,
        pltpu.VMEM((CX, CR, C3), BF16),
        pltpu.VMEM((FX, FR, C3), BF16),
        *halo_scratch(FR, (FR, C3)),
        *halo_scratch(32, (2, CR, C4)),
        *halo_scratch(32, (2, CR, C3)),
        *halo_scratch(FR, (FR, C3)),
        pltpu.VMEM((CX + 2, 32, C4), F32),
        pltpu.VMEM((128, C3), F32),
        pltpu.VMEM((512, C3), F32),
        pltpu.VMEM((6 * 32, C4), F32),
        pltpu.VMEM((64, C3), F32),
        pltpu.VMEM((512, C3), F32),
        pltpu.VMEM((128, C4), F32),
        pltpu.VMEM((16, 6 * 256), F32),
        pltpu.VMEM((144, 6 * 256), BF16),
        pltpu.VMEM((144, 6 * 256), BF16),
        pltpu.VMEM((2, 512, 128), F32),
        pltpu.VMEM((16 * 16, 128), F32),
        pltpu.VMEM((C4, 128), BF16),
        pltpu.VMEM((N, 16, 128), BF16),
        pltpu.VMEM((C4, 128), BF16),
        pltpu.VMEM((N, 16, 128), BF16),
        pltpu.VMEM((CX, N * CR, C3), BF16),
        pltpu.VMEM((CX, N * CR, C4), BF16),
        pltpu.VMEM((C3, 2 * HALF), F32),
        pltpu.VMEM((N, 16, HALF), BF16),
        pltpu.VMEM((N, 16, HALF), BF16),
        pltpu.VMEM((256, C3), F32),
        pltpu.VMEM((N, 16, 512), BF16),
        pltpu.VMEM((N, 16, 512), BF16),
        pltpu.VMEM((N, 16, 256), BF16),
        pltpu.VMEM((N, 16, 256), BF16),
        pltpu.VMEM((N, 16, 128), BF16),
        pltpu.VMEM((N, 16, 128), BF16),
        pltpu.SemaphoreType.DMA((5,)),
        pltpu.SemaphoreType.DMA((2,)),
        pltpu.SemaphoreType.DMA((2,)),
        pltpu.SemaphoreType.DMA((4, 8)),
        pltpu.SemaphoreType.DMA((4, 8)),
        pltpu.SemaphoreType.DMA((8, N)),
        pltpu.SemaphoreType.DMA((8, N)),
    ]
    shapes = (
            jax.ShapeDtypeStruct((FX, FR, C3), BF16),
            jax.ShapeDtypeStruct((8 * 8, 27), F32),
            jax.ShapeDtypeStruct((8 * 16, 27), F32),
            jax.ShapeDtypeStruct((16 * 16, 27), F32),
    )
    results = pl.pallas_call(
        kernel,
        out_shape=shapes,
        in_specs=[hbm] * 5,
        out_specs=(vmem, vmem, vmem, vmem),
        scratch_shapes=scratch,
        compiler_params=pltpu.CompilerParams(
            collective_id=0, has_side_effects=True, vmem_limit_bytes=61 * 1024 * 1024
        ),
        name="unet_backward",
    )(
        features.reshape(FX, FR, C3),
        cotangent,
        weight_fine,
        weight_down,
        weight_mid,
    )
    out_feat, out_fine, out_down, out_mid = pl.pallas_call(
        hand_over,
        out_shape=shapes,
        in_specs=[vmem] * 4,
        out_specs=(vmem,) * 4,
        name="hand_over",
    )(*results)
    return (
        out_feat.reshape(FX, FX, FZ, C3),
        out_fine.reshape(8, 8, 27).transpose(0, 2, 1),
        out_down.reshape(8, 16, 27).transpose(0, 2, 1),
        out_mid.reshape(16, 16, 27).transpose(0, 2, 1),
    )


def solution(mesh):
    in_specs = (P("gx", "gy", None, None), P(), P(), P(), P("gx", "gy", None, None))
    out_specs = (
        P("gx", "gy", None, None),
        P("gx", None, "gy"),
        P("gx", None, "gy"),
        P("gx", None, "gy"),
    )
    return jax.shard_map(
        per_device, mesh=mesh, in_specs=in_specs, out_specs=out_specs, check_vma=False
    )
```

```python
import math

import jax
import jax.numpy as jnp
from jax import lax
from jax.experimental import pallas as pl
from jax.experimental.pallas import tpu as pltpu
from jax.sharding import PartitionSpec as P

MESH = pl.DeviceIdType.MESH
F32 = jnp.float32
BF16 = jnp.bfloat16

N = 16
BASE = 8
FX, FZ, C3 = 8, 8, 128
CX, CZ, C4 = 4, 4, 256
FR, CR = FX * FZ, CX * CZ
HALF = 7 * C3

FEAT, COT, POOL, DF = range(4)
COT_T, POOL_G, ACT_G, DC_T, FINE, X_MID, X_DOWN, X_FINE = range(8)


def dot(a, b):
    return jnp.dot(a, b, preferred_element_type=F32)


def dot_t(a, b):
    return lax.dot_general(a, b, (((1,), (1,)), ((), ())), preferred_element_type=F32)


def kept(flag, value):
    return jnp.where(flag, value.astype(F32), 0.0)


def frame(reach):
    nx, nz = (FX, FZ) if reach == 1 else (CX, CZ)
    lo = BASE + 8
    return nx, lo, lo + nx * nz


def put_own(ext, own, reach):
    nx, lo, hi = frame(reach)
    ext[reach : reach + nx, lo:hi, :] = own


def pack(ext, send_y, send_c, reach):
    nx, lo, hi = frame(reach)
    chans = ext.shape[2]
    for side, start in ((0, lo), (1, hi - 8)):
        send_y[side] = ext[reach : reach + nx, start : start + 8, :].reshape(nx * 8, chans).astype(BF16)
        for end, x in ((0, reach), (1, nx)):
            if reach == 1:
                send_c[2 * end + side] = ext[x, start : start + 16, :].astype(BF16)
            else:
                send_c[2 * end + side] = ext[x : x + 2, start : start + 8, :].reshape(16, chans).astype(BF16)


def put_halo(ext, recv_x, recv_y, recv_c, inside, reach):
    nx, lo, hi = frame(reach)
    chans = ext.shape[2]
    for end, x in ((0, 0), (1, reach + nx)):
        ext[x : x + reach, lo:hi, :] = kept(inside[0][end], recv_x[end]).reshape(reach, hi - lo, chans)
    for side, start in ((0, lo - 8), (1, hi)):
        line = kept(inside[1][side], recv_y[side])
        ext[reach : reach + nx, start : start + 8, :] = line.reshape(nx, 8, chans)
        for end, x in ((0, 0), (1, reach + nx)):
            flag = jnp.logical_and(inside[0][end], inside[1][side])
            corner = kept(flag, recv_c[2 * end + side])[0 : 8 * reach]
            ext[x : x + reach, start : start + 8, :] = corner.reshape(reach, 8, chans)


def spread_lanes(ext, cols, nz):
    lo = BASE + nz
    rows = cols.shape[1]
    chans = ext.shape[2]
    z = lax.broadcasted_iota(jnp.int32, (rows, chans), 0) % nz

    def layer(x, carry):
        for b in range(3):
            for c in range(3):
                piece = ext[x, pl.ds(lo + nz * (b - 1) + c - 1, rows), :]
                if c == 0:
                    piece = jnp.where(z >= 1, piece, 0.0)
                if c == 2:
                    piece = jnp.where(z <= nz - 2, piece, 0.0)
                k = 3 * b + c
                cols[x, :, k * chans : (k + 1) * chans] = piece.astype(BF16)
        return carry

    lax.fori_loop(0, ext.shape[0], layer, 0)


def forward(cols, weight, nx):
    rows, depth = cols.shape[1], cols.shape[2]
    total = None
    for a in range(3):
        term = dot(
            cols[a : a + nx].reshape(nx * rows, depth),
            weight[9 * a : 9 * a + 9].reshape(depth, weight.shape[2]),
        )
        total = term if total is None else total + term
    return total


def backward(cols, weight, nx, total):
    rows = cols.shape[1]
    chans = weight.shape[2]
    for a in range(3):
        for k in range(9):
            piece = cols[a : a + nx, :, k * chans : (k + 1) * chans].reshape(nx * rows, chans)
            term = dot_t(piece, weight[26 - 9 * a - k])
            if a == 0 and k == 0:
                total[...] = term
            else:
                total[...] += term


def send_chunks(layers, flip, send_t):
    flip[0:96, :] = layers.reshape(96, C4)
    send_t[...] = flip[...].T.astype(BF16)


def gather_lanes(recv_t, lines, shifted):
    lane = lax.broadcasted_iota(jnp.int32, (16, 128), 1) // 16
    for t in range(2):
        pieces = [recv_t[8 * t + s].astype(F32) for s in range(8)]
        for x in range(6):
            tile = jnp.zeros((16, 128), F32)
            for s in range(8):
                moved = pltpu.roll(pieces[s], (16 * s - 16 * x) % 128, 1) if s != x else pieces[s]
                tile = jnp.where(lane == s, moved, tile)
            lines[:, 256 * x + 128 * t : 256 * x + 128 * t + 128] = tile
    width = 6 * 256
    place = lax.broadcasted_iota(jnp.int32, (16, width), 1)
    z = place % CZ
    y = (place % 256) // CZ
    whole = lines[...]
    for b in range(3):
        for c in range(3):
            step = CZ * (b - 1) + c - 1
            moved = pltpu.roll(whole, (-step) % width, 1) if step else whole
            keep = (z + (c - 1) >= 0) & (z + (c - 1) < CZ) & (y + (b - 1) >= 0) & (y + (b - 1) < 64)
            k = 3 * b + c
            shifted[16 * k : 16 * k + 16, :] = jnp.where(keep, moved, 0.0).astype(BF16)


def coarse_grad(shifted, field, out):
    chans = field.shape[2]
    cells = field[...].reshape(1024, chans)
    for a in range(3):
        term = dot(shifted[:, 256 * a : 256 * a + 1024], cells)
        for k in range(9):
            o = 26 - 9 * a - k
            for h in range(chans // 128):
                out[h, pl.ds(o, 16, stride=32), :] = term[16 * k : 16 * k + 16, 128 * h : 128 * h + 128]


def kernel(
    feat_hbm, cot_hbm, w_fine_hbm, w_down_hbm, w_mid_hbm,
    out_feat, out_fine, out_down, out_mid,
    feat, cot, own_c,
    w_fine, w_down, w_mid,
    ext_s, cols_s, border, border_s, turned_own, turned_s,
    ext_f, ext_c, ext_p, ext_d, ext_g,
    cols_f, cols_c, cols_p, cols_d, cols_g,
    own_p, own_g,
    sy_f, sc_f, rx_f, ry_f, rc_f,
    sy_c, sc_c, rx_c, ry_c, rc_c,
    sy_p, sc_p, rx_p, ry_p, rc_p,
    sy_g, sc_g, rx_g, ry_g, rc_g,
    act_c, pairs, slope_f, delta_act, delta_pool, total_f,
    flip, lines, shifted_c, shifted_d, wide, spread,
    st_c, rt_c, st_d, rt_d, all_p, all_a,
    part, send_f, recv_f, fold_f,
    sx_m, rx_m, sx_d, rx_d2, sx_f, rx_f2,
    w_sem, s_send, s_recv, h_send, h_recv, a_send, a_recv,
):
    mx, my = lax.axis_index("gx"), lax.axis_index("gy")

    def other(axis, step):
        if axis == 0:
            return (lax.rem(mx + step, N), my)
        return (mx, lax.rem(my + step, N))

    barrier = pltpu.get_barrier_semaphore()

    def greet(d, carry):
        for axis in range(2):
            pl.semaphore_signal(barrier, inc=1, device_id=other(axis, d), device_id_type=MESH)
        return carry

    lax.fori_loop(1, N, greet, 0)
    for dx in (1, N - 1):
        for dy in (1, N - 1):
            there = (lax.rem(mx + dx, N), lax.rem(my + dy, N))
            pl.semaphore_signal(barrier, inc=1, device_id=there, device_id_type=MESH)

    loads = [
        pltpu.make_async_copy(src, dst, w_sem.at[i])
        for i, (src, dst) in enumerate(
            (
                (feat_hbm, feat),
                (cot_hbm, cot),
                (w_fine_hbm, w_fine),
                (w_mid_hbm, w_mid),
                (w_down_hbm, w_down),
            )
        )
    ]
    for load in loads:
        load.start()

    inside = ((mx > 0, mx < N - 1), (my > 0, my < N - 1))

    def neighbours(kind, first, last, send_y, send_c, recv_x, recv_y, recv_c):
        copies = []

        def add(src, dst, dx, dy):
            slot = len(copies)
            copies.append(
                pltpu.make_async_remote_copy(
                    src_ref=src,
                    dst_ref=dst,
                    send_sem=h_send.at[kind, slot],
                    recv_sem=h_recv.at[kind, slot],
                    device_id=(lax.rem(mx + dx + N, N), lax.rem(my + dy + N, N)),
                    device_id_type=MESH,
                )
            )

        add(first, recv_x.at[1], -1, 0)
        add(last, recv_x.at[0], 1, 0)
        for side in range(2):
            add(send_y.at[side], recv_y.at[1 - side], 0, 2 * side - 1)
        for end in range(2):
            for side in range(2):
                i = 2 * end + side
                add(send_c.at[i], recv_c.at[3 - i], 2 * end - 1, 2 * side - 1)
        return copies

    def exchange(kind, axis, src, dst):
        me = (mx, my)[axis]

        def copy(d, slot):
            return pltpu.make_async_remote_copy(
                src_ref=src(lax.rem(me + d, N)),
                dst_ref=dst(slot),
                send_sem=a_send.at[kind, d],
                recv_sem=a_recv.at[kind, d],
                device_id=other(axis, d),
                device_id_type=MESH,
            )

        def start():
            def body(d, carry):
                copy(d, me).start()
                return carry

            lax.fori_loop(1, N, body, 0)

        def arrive():
            def body(d, carry):
                copy(d, lax.rem(me - d + N, N)).wait_recv()
                return carry

            lax.fori_loop(1, N, body, 0)

        def leave():
            def body(d, carry):
                copy(d, me).wait_send()
                return carry

            lax.fori_loop(1, N, body, 0)

        return start, arrive, leave

    def sixteen(i):
        return pl.ds(pl.multiple_of(16 * i, 16), 16)

    halo_f = neighbours(FEAT, feat.at[0], feat.at[FX - 1], sy_f, sc_f, rx_f, ry_f, rc_f)
    halo_c = neighbours(COT, own_c.at[0:2], own_c.at[CX - 2 : CX], sy_c, sc_c, rx_c, ry_c, rc_c)
    halo_p = neighbours(POOL, own_p.at[0:2], own_p.at[CX - 2 : CX], sy_p, sc_p, rx_p, ry_p, rc_p)
    halo_g = neighbours(DF, own_g.at[0], own_g.at[FX - 1], sy_g, sc_g, rx_g, ry_g, rc_g)
    move_ct = exchange(COT_T, 1, lambda t: st_c.at[sixteen(t)], lambda s: rt_c.at[s])
    move_dt = exchange(DC_T, 1, lambda t: st_d.at[sixteen(t)], lambda s: rt_d.at[s])
    move_p = exchange(POOL_G, 1, lambda t: all_p.at[:, sixteen(my)], lambda s: all_p.at[:, sixteen(s)])
    move_f = exchange(FINE, 1, lambda t: send_f.at[t], lambda s: recv_f.at[s])
    move_xm = exchange(X_MID, 0, lambda t: sx_m.at[t], lambda s: rx_m.at[s])
    move_xd = exchange(X_DOWN, 0, lambda t: sx_d.at[t], lambda s: rx_d2.at[s])
    move_xf = exchange(X_FINE, 0, lambda t: sx_f.at[t], lambda s: rx_f2.at[s])

    core = lax.rem(my, 2)
    sibling = (mx, my + 1 - 2 * core)

    def to_sibling(i, src, dst):
        return pltpu.make_async_remote_copy(
            src_ref=src,
            dst_ref=dst,
            send_sem=s_send.at[i],
            recv_sem=s_recv.at[i],
            device_id=sibling,
            device_id_type=MESH,
        )

    def block_a(slot, i, device):
        return pltpu.make_async_remote_copy(
            src_ref=all_a.at[:, sixteen(slot)],
            dst_ref=all_a.at[:, sixteen(slot)],
            send_sem=a_send.at[ACT_G, i],
            recv_sem=a_recv.at[ACT_G, i],
            device_id=device,
            device_id_type=MESH,
        )

    beside = sibling[1]

    def seven(step):
        def body(k, carry):
            step(k, lax.rem(my + 2 * k, N), lax.rem(my - 2 * k + N, N), lax.rem(beside - 2 * k + N, N))
            return carry

        lax.fori_loop(1, N // 2, body, 0)

    def start_a():
        block_a(my, 1, sibling).start()
        seven(lambda k, to, came, other_came: block_a(my, 2 * k, (mx, to)).start())

    def forward_a():
        def step(k, to, came, other_came):
            block_a(came, 2 * k, (mx, to)).wait_recv()
            block_a(came, 2 * k + 1, sibling).start()

        seven(step)

    def arrive_a():
        block_a(beside, 1, sibling).wait_recv()
        seven(lambda k, to, came, other_came: block_a(other_came, 2 * k + 1, sibling).wait_recv())

    def leave_a():
        block_a(my, 1, sibling).wait_send()

        def step(k, to, came, other_came):
            block_a(my, 2 * k, (mx, to)).wait_send()
            block_a(came, 2 * k + 1, sibling).wait_send()

        seven(step)

    sib_feat = to_sibling(0, border, border_s)
    sib_delta = to_sibling(1, turned_own, turned_s)

    loads[0].wait()
    put_own(ext_f, feat[...].astype(F32), 1)
    pack(ext_f, sy_f, sc_f, 1)
    pl.semaphore_wait(barrier, 2 * (N - 1) + 4)
    for copy in halo_f:
        copy.start()
    loads[1].wait()
    nx, lo, hi = frame(2)
    for x in range(CX):
        for y in range(CX):
            ext_c[2 + x, lo + CZ * y : lo + CZ * y + CZ, :] = cot[x, y].astype(F32)
    own_c[...] = ext_c[2 : CX + 2, lo:hi, :].astype(BF16)
    pack(ext_c, sy_c, sc_c, 2)
    for copy in halo_c:
        copy.start()

    for copy in halo_f:
        copy.wait_recv()
    put_halo(ext_f, rx_f, ry_f, rc_f, inside, 1)
    spread_lanes(ext_f, cols_f, FZ)
    loads[2].wait()
    pre = forward(cols_f, w_fine, FX)
    sig = jax.nn.sigmoid(pre)
    slope_f[...] = sig * (1.0 + pre * (1.0 - sig))
    act = (pre * sig).reshape(CX, 2, CX, 2, FZ, C3)
    pairs[...] = (act[:, 0, :, 0] + act[:, 0, :, 1] + act[:, 1, :, 0] + act[:, 1, :, 1]).reshape(128, C3)
    pooled = (pairs[pl.ds(0, 64, stride=2), :] + pairs[pl.ds(1, 64, stride=2), :]) * 0.125
    pooled = pooled.astype(BF16).reshape(CX, CR, C3)
    own_p[...] = pooled
    put_own(ext_p, pooled.astype(F32), 2)
    pack(ext_p, sy_p, sc_p, 2)
    for copy in halo_p:
        copy.start()
    border[...] = ext_f[:, BASE : BASE + FZ * (FX + 2), :].astype(BF16)
    sib_feat.start()
    all_p[:, sixteen(my), :] = pooled
    move_p[0]()

    for copy in halo_c:
        copy.wait_recv()
    put_halo(ext_c, rx_c, ry_c, rc_c, inside, 2)
    send_chunks(ext_c[1:7, lo:hi, :], flip, st_c)
    move_ct[0]()
    rt_c[my] = st_c[sixteen(my), :]
    spread_lanes(ext_c, cols_c, CZ)
    loads[3].wait()
    backward(cols_c, w_mid, CX + 2, delta_act)
    sib_feat.wait_recv()
    ext_s[:, BASE : BASE + FZ * (FX + 2), :] = border_s[...].astype(F32)
    spread_lanes(ext_s, cols_s, FZ)

    for copy in halo_p:
        copy.wait_recv()
    put_halo(ext_p, rx_p, ry_p, rc_p, inside, 2)
    spread_lanes(ext_p, cols_p, CZ)
    loads[4].wait()
    pre = forward(cols_p, w_down, CX + 2)
    sig = jax.nn.sigmoid(pre)
    act_c[...] = (pre * sig).reshape(CX + 2, 32, C4)
    all_a[:, sixteen(my), :] = act_c[1 : CX + 1, CZ : CZ + CR, :].astype(BF16)
    start_a()
    delta = (delta_act[...] * (sig * (1.0 + pre * (1.0 - sig)))).astype(BF16).astype(F32)
    last = BASE + CZ * (CX + 2)
    ext_d[:, BASE:last, :] = delta.reshape(CX + 2, 32, C4)[:, 0 : CZ * (CX + 2), :]
    for end, x in ((0, 0), (1, CX + 1)):
        ext_d[x, BASE:last, :] = kept(inside[0][end], ext_d[x, BASE:last, :])
    for side, start in ((0, BASE), (1, last - CZ)):
        ext_d[:, start : start + CZ, :] = kept(inside[1][side], ext_d[:, start : start + CZ, :])

    spread_lanes(ext_d, cols_d, CZ)
    backward(cols_d, w_down, CX, delta_pool)
    pooled_delta = delta_pool[...] * 0.125
    pairs[pl.ds(0, 64, stride=2), :] = pooled_delta
    pairs[pl.ds(1, 64, stride=2), :] = pooled_delta
    up = jnp.broadcast_to(pairs[...].reshape(CX, 1, CX, 1, FZ, C3), (CX, 2, CX, 2, FZ, C3))
    delta = (up.reshape(512, C3) * slope_f[...]).astype(BF16)
    turned_own[...] = delta.astype(F32).T.astype(BF16)
    sib_delta.start()
    send_chunks(ext_d[:, 12:28, :], flip, st_d)
    move_dt[0]()
    rt_d[my] = st_d[sixteen(my), :]

    lanes = pl.ds(pl.multiple_of(4 * C3 * core, C3), 5 * C3)

    def half(turned, cols):
        part[:, 0 : 9 * C3] += dot(turned, cols[pl.ds(2 * core, FX)].reshape(512, 9 * C3))
        part[:, 9 * C3 : 14 * C3] += dot(turned, cols[1 : 1 + FX, :, lanes].reshape(512, 5 * C3))

    part[...] = jnp.zeros(part.shape, F32)
    half(turned_own[...], cols_f)
    move_ct[1]()
    gather_lanes(rt_c, lines, shifted_c)

    sib_delta.wait_recv()
    half(turned_s[...], cols_s)

    def fold(j, carry):
        rows = pl.ds(pl.multiple_of(8 * j, 8), 8)
        send_f[j] = jnp.concatenate([part[rows, 0:HALF], part[rows, HALF : 2 * HALF]], axis=0).astype(BF16)
        return carry

    lax.fori_loop(0, N, fold, 0)
    move_f[0]()
    recv_f[my] = send_f[my]
    forward_a()
    own_g[...] = delta.reshape(FX, FR, C3)
    put_own(ext_g, delta.astype(F32).reshape(FX, FR, C3), 1)
    pack(ext_g, sy_g, sc_g, 1)
    for copy in halo_g:
        copy.start()

    arrive_a()
    coarse_grad(shifted_c, all_a, wide)
    for h in range(2):
        sx_m[8 * h : 8 * h + 8] = wide[h].T.astype(BF16).reshape(8, 16, 512)
    move_xm[0]()
    rx_m[mx] = sx_m[mx]

    move_dt[1]()
    gather_lanes(rt_d, lines, shifted_d)
    move_p[1]()
    coarse_grad(shifted_d, all_p, wide)
    turned = wide[0].T
    for i in range(N):
        rows = turned[8 * i : 8 * i + 8]
        sx_d[i] = jnp.concatenate([rows[:, 0:256], rows[:, 256:512]], axis=0).astype(BF16)
    move_xd[0]()
    rx_d2[mx] = sx_d[mx]

    move_f[1]()

    def add_f(s, totals):
        return tuple(totals[c] + recv_f[2 * s + c].astype(F32) for c in range(2))

    nothing = jnp.zeros((16, HALF), F32)
    totals = lax.fori_loop(0, N // 2, add_f, (nothing, nothing))
    for o in range(27):
        c, i = (0, o) if o < 14 else (1, o - 18 if o >= 18 else o - 4)
        half_at, at = divmod(i, 7)
        fold_f[pl.ds(o, 8, stride=32), :] = totals[c][8 * half_at : 8 * half_at + 8, C3 * at : C3 * at + C3]
    turned = fold_f[...].T
    for i in range(N):
        rows = turned[8 * i : 8 * i + 8]
        sx_f[i] = jnp.concatenate([rows[:, 0:128], rows[:, 128:256]], axis=0).astype(BF16)
    move_xf[0]()
    rx_f2[mx] = sx_f[mx]

    for copy in halo_g:
        copy.wait_recv()
    put_halo(ext_g, rx_g, ry_g, rc_g, inside, 1)
    spread_lanes(ext_g, cols_g, FZ)
    backward(cols_g, w_fine, FX, total_f)
    out_feat[...] = total_f[...].astype(BF16).reshape(FX, FR, C3)

    def summed(arrived):
        def add(s, total):
            return total + arrived[s].astype(F32)

        return lax.fori_loop(0, N, add, jnp.zeros(arrived.shape[1:], F32))

    def unfold(out, total, rows, first, most):
        for co in range(first, first + most):
            at = 32 * (co - first)
            spread[pl.ds(co, rows, stride=out.shape[0] // rows), 0:32] = total[:, at : at + 32]
        out[...] = spread[0 : out.shape[0], 0:27]

    coarse_scale = 1.0 / math.sqrt(CX * N * CX * N * CZ)
    move_xm[1]()
    unfold(out_mid, summed(rx_m) * coarse_scale, 16, 0, 16)
    move_xd[1]()
    total = summed(rx_d2) * coarse_scale
    unfold(out_down, total[0:8], 8, 0, 8)
    unfold(out_down, total[8:16], 8, 8, 8)
    move_xf[1]()
    total = summed(rx_f2) * (1.0 / math.sqrt(FX * N * FX * N * FZ))
    unfold(out_fine, total[0:8], 8, 0, 4)
    unfold(out_fine, total[8:16], 8, 4, 4)

    for copy in halo_f + halo_c + halo_p + halo_g + [sib_feat, sib_delta]:
        copy.wait_send()
    leave_a()
    for move in (move_ct, move_dt, move_p, move_f, move_xm, move_xd, move_xf):
        move[2]()


def halo_scratch(lines, layers):
    chans = layers[-1]
    return [
        pltpu.VMEM((2, lines, chans), BF16),
        pltpu.VMEM((4, 16, chans), BF16),
        pltpu.VMEM((2, *layers), BF16),
        pltpu.VMEM((2, lines, chans), BF16),
        pltpu.VMEM((4, 16, chans), BF16),
    ]


def hand_over(*refs):
    for i in range(4):
        refs[4 + i][...] = refs[i][...]


def per_device(features, weight_fine, weight_down, weight_mid, cotangent):
    vmem = pl.BlockSpec(memory_space=pltpu.VMEM)
    hbm = pl.BlockSpec(memory_space=pltpu.HBM)
    fine_ext = pltpu.VMEM((FX + 2, 2 * BASE + FZ * (FX + 2), C3), F32)
    fine_cols = pltpu.VMEM((FX + 2, FR, 9 * C3), BF16)

    def wide_ext(chans):
        return pltpu.VMEM((CX + 4, 3 * BASE + CZ * (CX + 4), chans), F32)

    def wide_cols(chans):
        return pltpu.VMEM((CX + 4, 32, 9 * chans), BF16)

    ext_d = pltpu.VMEM((CX + 2, 2 * BASE + CZ * (CX + 2), C4), F32)
    cols_d = pltpu.VMEM((CX + 2, CR, 9 * C4), BF16)

    scratch = [
        pltpu.VMEM((FX, FR, C3), BF16),
        pltpu.VMEM((CX, CX, CZ, C4), BF16),
        pltpu.VMEM((CX, CR, C4), BF16),
        pltpu.VMEM((27, C3, C3), BF16),
        pltpu.VMEM((27, C3, C4), BF16),
        pltpu.VMEM((27, C4, C4), BF16),
        fine_ext, fine_cols,
        pltpu.VMEM((FX + 2, FZ * (FX + 2), C3), BF16),
        pltpu.VMEM((FX + 2, FZ * (FX + 2), C3), BF16),
        pltpu.VMEM((C3, 512), BF16),
        pltpu.VMEM((C3, 512), BF16),
        fine_ext, wide_ext(C4), wide_ext(C3), ext_d, fine_ext,
        fine_cols, wide_cols(C4), wide_cols(C3), cols_d, fine_cols,
        pltpu.VMEM((CX, CR, C3), BF16),
        pltpu.VMEM((FX, FR, C3), BF16),
        *halo_scratch(FR, (FR, C3)),
        *halo_scratch(32, (2, CR, C4)),
        *halo_scratch(32, (2, CR, C3)),
        *halo_scratch(FR, (FR, C3)),
        pltpu.VMEM((CX + 2, 32, C4), F32),
        pltpu.VMEM((128, C3), F32),
        pltpu.VMEM((512, C3), F32),
        pltpu.VMEM((6 * 32, C4), F32),
        pltpu.VMEM((64, C3), F32),
        pltpu.VMEM((512, C3), F32),
        pltpu.VMEM((128, C4), F32),
        pltpu.VMEM((16, 6 * 256), F32),
        pltpu.VMEM((144, 6 * 256), BF16),
        pltpu.VMEM((144, 6 * 256), BF16),
        pltpu.VMEM((2, 512, 128), F32),
        pltpu.VMEM((16 * 16, 128), F32),
        pltpu.VMEM((C4, 128), BF16),
        pltpu.VMEM((N, 16, 128), BF16),
        pltpu.VMEM((C4, 128), BF16),
        pltpu.VMEM((N, 16, 128), BF16),
        pltpu.VMEM((CX, N * CR, C3), BF16),
        pltpu.VMEM((CX, N * CR, C4), BF16),
        pltpu.VMEM((C3, 2 * HALF), F32),
        pltpu.VMEM((N, 16, HALF), BF16),
        pltpu.VMEM((N, 16, HALF), BF16),
        pltpu.VMEM((256, C3), F32),
        pltpu.VMEM((N, 16, 512), BF16),
        pltpu.VMEM((N, 16, 512), BF16),
        pltpu.VMEM((N, 16, 256), BF16),
        pltpu.VMEM((N, 16, 256), BF16),
        pltpu.VMEM((N, 16, 128), BF16),
        pltpu.VMEM((N, 16, 128), BF16),
        pltpu.SemaphoreType.DMA((5,)),
        pltpu.SemaphoreType.DMA((2,)),
        pltpu.SemaphoreType.DMA((2,)),
        pltpu.SemaphoreType.DMA((4, 8)),
        pltpu.SemaphoreType.DMA((4, 8)),
        pltpu.SemaphoreType.DMA((8, N)),
        pltpu.SemaphoreType.DMA((8, N)),
    ]
    shapes = (
            jax.ShapeDtypeStruct((FX, FR, C3), BF16),
            jax.ShapeDtypeStruct((8 * 8, 27), F32),
            jax.ShapeDtypeStruct((8 * 16, 27), F32),
            jax.ShapeDtypeStruct((16 * 16, 27), F32),
    )
    results = pl.pallas_call(
        kernel,
        out_shape=shapes,
        in_specs=[hbm] * 5,
        out_specs=(vmem, vmem, vmem, vmem),
        scratch_shapes=scratch,
        compiler_params=pltpu.CompilerParams(
            collective_id=0, has_side_effects=True, vmem_limit_bytes=61 * 1024 * 1024
        ),
        name="unet_backward",
    )(
        features.reshape(FX, FR, C3),
        cotangent,
        weight_fine,
        weight_down,
        weight_mid,
    )
    out_feat, out_fine, out_down, out_mid = pl.pallas_call(
        hand_over,
        out_shape=shapes,
        in_specs=[vmem] * 4,
        out_specs=(vmem,) * 4,
        name="hand_over",
    )(*results)
    return (
        out_feat.reshape(FX, FX, FZ, C3),
        out_fine.reshape(8, 8, 27).transpose(0, 2, 1),
        out_down.reshape(8, 16, 27).transpose(0, 2, 1),
        out_mid.reshape(16, 16, 27).transpose(0, 2, 1),
    )


def solution(mesh):
    in_specs = (P("gx", "gy", None, None), P(), P(), P(), P("gx", "gy", None, None))
    out_specs = (
        P("gx", "gy", None, None),
        P("gx", None, "gy"),
        P("gx", None, "gy"),
        P("gx", None, "gy"),
    )
    return jax.shard_map(
        per_device, mesh=mesh, in_specs=in_specs, out_specs=out_specs, check_vma=False
    )
```

```python
import math

import jax
import jax.numpy as jnp
from jax import lax
from jax.experimental import pallas as pl
from jax.experimental.pallas import tpu as pltpu
from jax.sharding import PartitionSpec as P

MESH = pl.DeviceIdType.MESH
F32 = jnp.float32
BF16 = jnp.bfloat16

N = 16
BASE = 8
FX, FZ, C3 = 8, 8, 128
CX, CZ, C4 = 4, 4, 256
FR, CR = FX * FZ, CX * CZ
HALF = 7 * C3

FEAT, COT, POOL, DF = range(4)
COT_T, POOL_G, ACT_G, DC_T, FINE, X_MID, X_DOWN, X_FINE = range(8)


def dot(a, b):
    return jnp.dot(a, b, preferred_element_type=F32)


def dot_t(a, b):
    return lax.dot_general(a, b, (((1,), (1,)), ((), ())), preferred_element_type=F32)


def kept(flag, value):
    return jnp.where(flag, value.astype(F32), 0.0)


def frame(reach):
    nx, nz = (FX, FZ) if reach == 1 else (CX, CZ)
    lo = BASE + 8
    return nx, lo, lo + nx * nz


def put_own(ext, own, reach):
    nx, lo, hi = frame(reach)
    ext[reach : reach + nx, lo:hi, :] = own


def pack(ext, send_y, send_c, reach):
    nx, lo, hi = frame(reach)
    chans = ext.shape[2]
    for side, start in ((0, lo), (1, hi - 8)):
        send_y[side] = ext[reach : reach + nx, start : start + 8, :].reshape(nx * 8, chans).astype(BF16)
        for end, x in ((0, reach), (1, nx)):
            if reach == 1:
                send_c[2 * end + side] = ext[x, start : start + 16, :].astype(BF16)
            else:
                send_c[2 * end + side] = ext[x : x + 2, start : start + 8, :].reshape(16, chans).astype(BF16)


def put_halo(ext, recv_x, recv_y, recv_c, inside, reach):
    nx, lo, hi = frame(reach)
    chans = ext.shape[2]
    for end, x in ((0, 0), (1, reach + nx)):
        ext[x : x + reach, lo:hi, :] = kept(inside[0][end], recv_x[end]).reshape(reach, hi - lo, chans)
    for side, start in ((0, lo - 8), (1, hi)):
        line = kept(inside[1][side], recv_y[side])
        ext[reach : reach + nx, start : start + 8, :] = line.reshape(nx, 8, chans)
        for end, x in ((0, 0), (1, reach + nx)):
            flag = jnp.logical_and(inside[0][end], inside[1][side])
            corner = kept(flag, recv_c[2 * end + side])[0 : 8 * reach]
            ext[x : x + reach, start : start + 8, :] = corner.reshape(reach, 8, chans)


def spread_lanes(ext, cols, nz):
    lo = BASE + nz
    rows = cols.shape[1]
    chans = ext.shape[2]
    z = lax.broadcasted_iota(jnp.int32, (rows, chans), 0) % nz

    def layer(x, carry):
        for b in range(3):
            for c in range(3):
                piece = ext[x, pl.ds(lo + nz * (b - 1) + c - 1, rows), :]
                if c == 0:
                    piece = jnp.where(z >= 1, piece, 0.0)
                if c == 2:
                    piece = jnp.where(z <= nz - 2, piece, 0.0)
                k = 3 * b + c
                cols[x, :, k * chans : (k + 1) * chans] = piece.astype(BF16)
        return carry

    lax.fori_loop(0, ext.shape[0], layer, 0)


def forward(cols, weight, nx):
    rows, depth = cols.shape[1], cols.shape[2]
    total = None
    for a in range(3):
        term = dot(
            cols[a : a + nx].reshape(nx * rows, depth),
            weight[9 * a : 9 * a + 9].reshape(depth, weight.shape[2]),
        )
        total = term if total is None else total + term
    return total


def backward(cols, weight, nx, total):
    rows = cols.shape[1]
    chans = weight.shape[2]
    for a in range(3):
        for k in range(9):
            piece = cols[a : a + nx, :, k * chans : (k + 1) * chans].reshape(nx * rows, chans)
            term = dot_t(piece, weight[26 - 9 * a - k])
            if a == 0 and k == 0:
                total[...] = term
            else:
                total[...] += term


def send_chunks(layers, flip, send_t):
    flip[0:96, :] = layers.reshape(96, C4)
    send_t[...] = flip[...].T.astype(BF16)


def gather_lanes(recv_t, lines, shifted):
    lane = lax.broadcasted_iota(jnp.int32, (16, 128), 1) // 16
    for t in range(2):
        pieces = [recv_t[8 * t + s].astype(F32) for s in range(8)]
        for x in range(6):
            tile = jnp.zeros((16, 128), F32)
            for s in range(8):
                moved = pltpu.roll(pieces[s], (16 * s - 16 * x) % 128, 1) if s != x else pieces[s]
                tile = jnp.where(lane == s, moved, tile)
            lines[:, 256 * x + 128 * t : 256 * x + 128 * t + 128] = tile
    width = 6 * 256
    place = lax.broadcasted_iota(jnp.int32, (16, width), 1)
    z = place % CZ
    y = (place % 256) // CZ
    whole = lines[...]
    for b in range(3):
        for c in range(3):
            step = CZ * (b - 1) + c - 1
            moved = pltpu.roll(whole, (-step) % width, 1) if step else whole
            keep = (z + (c - 1) >= 0) & (z + (c - 1) < CZ) & (y + (b - 1) >= 0) & (y + (b - 1) < 64)
            k = 3 * b + c
            shifted[16 * k : 16 * k + 16, :] = jnp.where(keep, moved, 0.0).astype(BF16)


def coarse_grad(shifted, field, out):
    chans = field.shape[2]
    cells = field[...].reshape(1024, chans)
    for a in range(3):
        term = dot(shifted[:, 256 * a : 256 * a + 1024], cells)
        for k in range(9):
            o = 26 - 9 * a - k
            for h in range(chans // 128):
                out[h, pl.ds(o, 16, stride=32), :] = term[16 * k : 16 * k + 16, 128 * h : 128 * h + 128]


def kernel(
    feat_hbm, cot_hbm, w_fine_hbm, w_down_hbm, w_mid_hbm,
    out_feat, out_fine, out_down, out_mid,
    feat, cot, own_c,
    w_fine, w_down, w_mid,
    ext_s, cols_s, border, border_s, turned_own, turned_s,
    ext_f, ext_c, ext_p, ext_d, ext_g,
    cols_f, cols_c, cols_p, cols_d, cols_g,
    own_p, own_g,
    sy_f, sc_f, rx_f, ry_f, rc_f,
    sy_c, sc_c, rx_c, ry_c, rc_c,
    sy_p, sc_p, rx_p, ry_p, rc_p,
    sy_g, sc_g, rx_g, ry_g, rc_g,
    act_c, pairs, slope_f, delta_act, delta_pool, total_f,
    flip, lines, shifted_c, shifted_d, wide, spread,
    st_c, rt_c, st_d, rt_d, all_p, all_a,
    part, send_f, recv_f, fold_f,
    sx_m, rx_m, sx_d, rx_d2, sx_f, rx_f2,
    w_sem, s_send, s_recv, h_send, h_recv, a_send, a_recv,
):
    mx, my = lax.axis_index("gx"), lax.axis_index("gy")

    def other(axis, step):
        if axis == 0:
            return (lax.rem(mx + step, N), my)
        return (mx, lax.rem(my + step, N))

    barrier = pltpu.get_barrier_semaphore()

    def greet(d, carry):
        for axis in range(2):
            pl.semaphore_signal(barrier, inc=1, device_id=other(axis, d), device_id_type=MESH)
        return carry

    lax.fori_loop(1, N, greet, 0)
    for dx in (1, N - 1):
        for dy in (1, N - 1):
            there = (lax.rem(mx + dx, N), lax.rem(my + dy, N))
            pl.semaphore_signal(barrier, inc=1, device_id=there, device_id_type=MESH)

    loads = [
        pltpu.make_async_copy(src, dst, w_sem.at[i])
        for i, (src, dst) in enumerate(
            (
                (feat_hbm, feat),
                (cot_hbm, cot),
                (w_fine_hbm, w_fine),
                (w_mid_hbm, w_mid),
                (w_down_hbm, w_down),
            )
        )
    ]
    for load in loads:
        load.start()

    inside = ((mx > 0, mx < N - 1), (my > 0, my < N - 1))

    def neighbours(kind, first, last, send_y, send_c, recv_x, recv_y, recv_c):
        copies = []

        def add(src, dst, dx, dy):
            slot = len(copies)
            copies.append(
                pltpu.make_async_remote_copy(
                    src_ref=src,
                    dst_ref=dst,
                    send_sem=h_send.at[kind, slot],
                    recv_sem=h_recv.at[kind, slot],
                    device_id=(lax.rem(mx + dx + N, N), lax.rem(my + dy + N, N)),
                    device_id_type=MESH,
                )
            )

        add(first, recv_x.at[1], -1, 0)
        add(last, recv_x.at[0], 1, 0)
        for side in range(2):
            add(send_y.at[side], recv_y.at[1 - side], 0, 2 * side - 1)
        for end in range(2):
            for side in range(2):
                i = 2 * end + side
                add(send_c.at[i], recv_c.at[3 - i], 2 * end - 1, 2 * side - 1)
        return copies

    def exchange(kind, axis, src, dst):
        me = (mx, my)[axis]

        def copy(d, slot):
            return pltpu.make_async_remote_copy(
                src_ref=src(lax.rem(me + d, N)),
                dst_ref=dst(slot),
                send_sem=a_send.at[kind, d],
                recv_sem=a_recv.at[kind, d],
                device_id=other(axis, d),
                device_id_type=MESH,
            )

        def start():
            def body(d, carry):
                copy(d, me).start()
                return carry

            lax.fori_loop(1, N, body, 0)

        def arrive():
            def body(d, carry):
                copy(d, lax.rem(me - d + N, N)).wait_recv()
                return carry

            lax.fori_loop(1, N, body, 0)

        def leave():
            def body(d, carry):
                copy(d, me).wait_send()
                return carry

            lax.fori_loop(1, N, body, 0)

        return start, arrive, leave

    def sixteen(i):
        return pl.ds(pl.multiple_of(16 * i, 16), 16)

    halo_f = neighbours(FEAT, feat.at[0], feat.at[FX - 1], sy_f, sc_f, rx_f, ry_f, rc_f)
    halo_c = neighbours(COT, own_c.at[0:2], own_c.at[CX - 2 : CX], sy_c, sc_c, rx_c, ry_c, rc_c)
    halo_p = neighbours(POOL, own_p.at[0:2], own_p.at[CX - 2 : CX], sy_p, sc_p, rx_p, ry_p, rc_p)
    halo_g = neighbours(DF, own_g.at[0], own_g.at[FX - 1], sy_g, sc_g, rx_g, ry_g, rc_g)
    move_ct = exchange(COT_T, 1, lambda t: st_c.at[sixteen(t)], lambda s: rt_c.at[s])
    move_dt = exchange(DC_T, 1, lambda t: st_d.at[sixteen(t)], lambda s: rt_d.at[s])
    move_p = exchange(POOL_G, 1, lambda t: all_p.at[:, sixteen(my)], lambda s: all_p.at[:, sixteen(s)])
    move_f = exchange(FINE, 1, lambda t: send_f.at[t], lambda s: recv_f.at[s])
    move_xm = exchange(X_MID, 0, lambda t: sx_m.at[t], lambda s: rx_m.at[s])
    move_xd = exchange(X_DOWN, 0, lambda t: sx_d.at[t], lambda s: rx_d2.at[s])
    move_xf = exchange(X_FINE, 0, lambda t: sx_f.at[t], lambda s: rx_f2.at[s])

    core = lax.rem(my, 2)
    sibling = (mx, my + 1 - 2 * core)

    def to_sibling(i, src, dst):
        return pltpu.make_async_remote_copy(
            src_ref=src,
            dst_ref=dst,
            send_sem=s_send.at[i],
            recv_sem=s_recv.at[i],
            device_id=sibling,
            device_id_type=MESH,
        )

    def block_a(slot, i, device):
        return pltpu.make_async_remote_copy(
            src_ref=all_a.at[:, sixteen(slot)],
            dst_ref=all_a.at[:, sixteen(slot)],
            send_sem=a_send.at[ACT_G, i],
            recv_sem=a_recv.at[ACT_G, i],
            device_id=device,
            device_id_type=MESH,
        )

    beside = sibling[1]

    def seven(step):
        def body(k, carry):
            step(k, lax.rem(my + 2 * k, N), lax.rem(my - 2 * k + N, N), lax.rem(beside - 2 * k + N, N))
            return carry

        lax.fori_loop(1, N // 2, body, 0)

    def start_a():
        block_a(my, 1, sibling).start()
        seven(lambda k, to, came, other_came: block_a(my, 2 * k, (mx, to)).start())

    def forward_a():
        def step(k, to, came, other_came):
            block_a(came, 2 * k, (mx, to)).wait_recv()
            block_a(came, 2 * k + 1, sibling).start()

        seven(step)

    def arrive_a():
        block_a(beside, 1, sibling).wait_recv()
        seven(lambda k, to, came, other_came: block_a(other_came, 2 * k + 1, sibling).wait_recv())

    def leave_a():
        block_a(my, 1, sibling).wait_send()

        def step(k, to, came, other_came):
            block_a(my, 2 * k, (mx, to)).wait_send()
            block_a(came, 2 * k + 1, sibling).wait_send()

        seven(step)

    sib_feat = to_sibling(0, border, border_s)
    sib_delta = to_sibling(1, turned_own, turned_s)

    loads[0].wait()
    put_own(ext_f, feat[...].astype(F32), 1)
    pack(ext_f, sy_f, sc_f, 1)
    pl.semaphore_wait(barrier, 2 * (N - 1) + 4)
    for copy in halo_f:
        copy.start()
    loads[1].wait()
    nx, lo, hi = frame(2)
    for x in range(CX):
        for y in range(CX):
            ext_c[2 + x, lo + CZ * y : lo + CZ * y + CZ, :] = cot[x, y].astype(F32)
    own_c[...] = ext_c[2 : CX + 2, lo:hi, :].astype(BF16)
    pack(ext_c, sy_c, sc_c, 2)
    for copy in halo_c:
        copy.start()

    for copy in halo_f:
        copy.wait_recv()
    put_halo(ext_f, rx_f, ry_f, rc_f, inside, 1)
    spread_lanes(ext_f, cols_f, FZ)
    loads[2].wait()
    pre = forward(cols_f, w_fine, FX)
    sig = jax.nn.sigmoid(pre)
    slope_f[...] = sig * (1.0 + pre * (1.0 - sig))
    act = (pre * sig).reshape(CX, 2, CX, 2, FZ, C3)
    pairs[...] = (act[:, 0, :, 0] + act[:, 0, :, 1] + act[:, 1, :, 0] + act[:, 1, :, 1]).reshape(128, C3)
    pooled = (pairs[pl.ds(0, 64, stride=2), :] + pairs[pl.ds(1, 64, stride=2), :]) * 0.125
    pooled = pooled.astype(BF16).reshape(CX, CR, C3)
    own_p[...] = pooled
    put_own(ext_p, pooled.astype(F32), 2)
    pack(ext_p, sy_p, sc_p, 2)
    for copy in halo_p:
        copy.start()
    border[...] = ext_f[:, BASE : BASE + FZ * (FX + 2), :].astype(BF16)
    sib_feat.start()
    all_p[:, sixteen(my), :] = pooled
    move_p[0]()

    for copy in halo_c:
        copy.wait_recv()
    put_halo(ext_c, rx_c, ry_c, rc_c, inside, 2)
    send_chunks(ext_c[1:7, lo:hi, :], flip, st_c)
    move_ct[0]()
    rt_c[my] = st_c[sixteen(my), :]
    spread_lanes(ext_c, cols_c, CZ)
    loads[3].wait()
    backward(cols_c, w_mid, CX + 2, delta_act)
    sib_feat.wait_recv()
    ext_s[:, BASE : BASE + FZ * (FX + 2), :] = border_s[...].astype(F32)
    spread_lanes(ext_s, cols_s, FZ)

    for copy in halo_p:
        copy.wait_recv()
    put_halo(ext_p, rx_p, ry_p, rc_p, inside, 2)
    spread_lanes(ext_p, cols_p, CZ)
    loads[4].wait()
    pre = forward(cols_p, w_down, CX + 2)
    sig = jax.nn.sigmoid(pre)
    act_c[...] = (pre * sig).reshape(CX + 2, 32, C4)
    all_a[:, sixteen(my), :] = act_c[1 : CX + 1, CZ : CZ + CR, :].astype(BF16)
    start_a()
    delta = (delta_act[...] * (sig * (1.0 + pre * (1.0 - sig)))).astype(BF16).astype(F32)
    last = BASE + CZ * (CX + 2)
    ext_d[:, BASE:last, :] = delta.reshape(CX + 2, 32, C4)[:, 0 : CZ * (CX + 2), :]
    for end, x in ((0, 0), (1, CX + 1)):
        ext_d[x, BASE:last, :] = kept(inside[0][end], ext_d[x, BASE:last, :])
    for side, start in ((0, BASE), (1, last - CZ)):
        ext_d[:, start : start + CZ, :] = kept(inside[1][side], ext_d[:, start : start + CZ, :])

    spread_lanes(ext_d, cols_d, CZ)
    backward(cols_d, w_down, CX, delta_pool)
    pooled_delta = delta_pool[...] * 0.125
    pairs[pl.ds(0, 64, stride=2), :] = pooled_delta
    pairs[pl.ds(1, 64, stride=2), :] = pooled_delta
    up = jnp.broadcast_to(pairs[...].reshape(CX, 1, CX, 1, FZ, C3), (CX, 2, CX, 2, FZ, C3))
    delta = (up.reshape(512, C3) * slope_f[...]).astype(BF16)
    turned_own[...] = delta.astype(F32).T.astype(BF16)
    sib_delta.start()
    send_chunks(ext_d[:, 12:28, :], flip, st_d)
    move_dt[0]()
    rt_d[my] = st_d[sixteen(my), :]

    lanes = pl.ds(pl.multiple_of(4 * C3 * core, C3), 5 * C3)

    def half(turned, cols):
        part[:, 0 : 9 * C3] += dot(turned, cols[pl.ds(2 * core, FX)].reshape(512, 9 * C3))
        part[:, 9 * C3 : 14 * C3] += dot(turned, cols[1 : 1 + FX, :, lanes].reshape(512, 5 * C3))

    part[...] = jnp.zeros(part.shape, F32)
    half(turned_own[...], cols_f)
    move_ct[1]()
    gather_lanes(rt_c, lines, shifted_c)

    sib_delta.wait_recv()
    half(turned_s[...], cols_s)

    def fold(j, carry):
        rows = pl.ds(pl.multiple_of(8 * j, 8), 8)
        send_f[j] = jnp.concatenate([part[rows, 0:HALF], part[rows, HALF : 2 * HALF]], axis=0).astype(BF16)
        return carry

    lax.fori_loop(0, N, fold, 0)
    move_f[0]()
    recv_f[my] = send_f[my]
    forward_a()
    own_g[...] = delta.reshape(FX, FR, C3)
    put_own(ext_g, delta.astype(F32).reshape(FX, FR, C3), 1)
    pack(ext_g, sy_g, sc_g, 1)
    for copy in halo_g:
        copy.start()

    move_dt[1]()
    gather_lanes(rt_d, lines, shifted_d)
    move_p[1]()
    coarse_grad(shifted_d, all_p, wide)
    turned = wide[0].T
    for i in range(N):
        rows = turned[8 * i : 8 * i + 8]
        sx_d[i] = jnp.concatenate([rows[:, 0:256], rows[:, 256:512]], axis=0).astype(BF16)
    move_xd[0]()
    rx_d2[mx] = sx_d[mx]

    arrive_a()
    coarse_grad(shifted_c, all_a, wide)
    for h in range(2):
        sx_m[8 * h : 8 * h + 8] = wide[h].T.astype(BF16).reshape(8, 16, 512)
    move_xm[0]()
    rx_m[mx] = sx_m[mx]

    move_f[1]()

    def add_f(s, totals):
        return tuple(totals[c] + recv_f[2 * s + c].astype(F32) for c in range(2))

    nothing = jnp.zeros((16, HALF), F32)
    totals = lax.fori_loop(0, N // 2, add_f, (nothing, nothing))
    for o in range(27):
        c, i = (0, o) if o < 14 else (1, o - 18 if o >= 18 else o - 4)
        half_at, at = divmod(i, 7)
        fold_f[pl.ds(o, 8, stride=32), :] = totals[c][8 * half_at : 8 * half_at + 8, C3 * at : C3 * at + C3]
    turned = fold_f[...].T
    for i in range(N):
        rows = turned[8 * i : 8 * i + 8]
        sx_f[i] = jnp.concatenate([rows[:, 0:128], rows[:, 128:256]], axis=0).astype(BF16)
    move_xf[0]()
    rx_f2[mx] = sx_f[mx]

    for copy in halo_g:
        copy.wait_recv()
    put_halo(ext_g, rx_g, ry_g, rc_g, inside, 1)
    spread_lanes(ext_g, cols_g, FZ)
    backward(cols_g, w_fine, FX, total_f)
    out_feat[...] = total_f[...].astype(BF16).reshape(FX, FR, C3)

    def summed(arrived):
        def add(s, total):
            return total + arrived[s].astype(F32)

        return lax.fori_loop(0, N, add, jnp.zeros(arrived.shape[1:], F32))

    def unfold(out, total, rows, first, most):
        for co in range(first, first + most):
            at = 32 * (co - first)
            spread[pl.ds(co, rows, stride=out.shape[0] // rows), 0:32] = total[:, at : at + 32]
        out[...] = spread[0 : out.shape[0], 0:27]

    coarse_scale = 1.0 / math.sqrt(CX * N * CX * N * CZ)
    move_xm[1]()
    unfold(out_mid, summed(rx_m) * coarse_scale, 16, 0, 16)
    move_xd[1]()
    total = summed(rx_d2) * coarse_scale
    unfold(out_down, total[0:8], 8, 0, 8)
    unfold(out_down, total[8:16], 8, 8, 8)
    move_xf[1]()
    total = summed(rx_f2) * (1.0 / math.sqrt(FX * N * FX * N * FZ))
    unfold(out_fine, total[0:8], 8, 0, 4)
    unfold(out_fine, total[8:16], 8, 4, 4)

    for copy in halo_f + halo_c + halo_p + halo_g + [sib_feat, sib_delta]:
        copy.wait_send()
    leave_a()
    for move in (move_ct, move_dt, move_p, move_f, move_xm, move_xd, move_xf):
        move[2]()


def halo_scratch(lines, layers):
    chans = layers[-1]
    return [
        pltpu.VMEM((2, lines, chans), BF16),
        pltpu.VMEM((4, 16, chans), BF16),
        pltpu.VMEM((2, *layers), BF16),
        pltpu.VMEM((2, lines, chans), BF16),
        pltpu.VMEM((4, 16, chans), BF16),
    ]


def hand_over(*refs):
    for i in range(4):
        refs[4 + i][...] = refs[i][...]


def per_device(features, weight_fine, weight_down, weight_mid, cotangent):
    vmem = pl.BlockSpec(memory_space=pltpu.VMEM)
    hbm = pl.BlockSpec(memory_space=pltpu.HBM)
    fine_ext = pltpu.VMEM((FX + 2, 2 * BASE + FZ * (FX + 2), C3), F32)
    fine_cols = pltpu.VMEM((FX + 2, FR, 9 * C3), BF16)

    def wide_ext(chans):
        return pltpu.VMEM((CX + 4, 3 * BASE + CZ * (CX + 4), chans), F32)

    def wide_cols(chans):
        return pltpu.VMEM((CX + 4, 32, 9 * chans), BF16)

    ext_d = pltpu.VMEM((CX + 2, 2 * BASE + CZ * (CX + 2), C4), F32)
    cols_d = pltpu.VMEM((CX + 2, CR, 9 * C4), BF16)

    scratch = [
        pltpu.VMEM((FX, FR, C3), BF16),
        pltpu.VMEM((CX, CX, CZ, C4), BF16),
        pltpu.VMEM((CX, CR, C4), BF16),
        pltpu.VMEM((27, C3, C3), BF16),
        pltpu.VMEM((27, C3, C4), BF16),
        pltpu.VMEM((27, C4, C4), BF16),
        fine_ext, fine_cols,
        pltpu.VMEM((FX + 2, FZ * (FX + 2), C3), BF16),
        pltpu.VMEM((FX + 2, FZ * (FX + 2), C3), BF16),
        pltpu.VMEM((C3, 512), BF16),
        pltpu.VMEM((C3, 512), BF16),
        fine_ext, wide_ext(C4), wide_ext(C3), ext_d, fine_ext,
        fine_cols, wide_cols(C4), wide_cols(C3), cols_d, fine_cols,
        pltpu.VMEM((CX, CR, C3), BF16),
        pltpu.VMEM((FX, FR, C3), BF16),
        *halo_scratch(FR, (FR, C3)),
        *halo_scratch(32, (2, CR, C4)),
        *halo_scratch(32, (2, CR, C3)),
        *halo_scratch(FR, (FR, C3)),
        pltpu.VMEM((CX + 2, 32, C4), F32),
        pltpu.VMEM((128, C3), F32),
        pltpu.VMEM((512, C3), F32),
        pltpu.VMEM((6 * 32, C4), F32),
        pltpu.VMEM((64, C3), F32),
        pltpu.VMEM((512, C3), F32),
        pltpu.VMEM((128, C4), F32),
        pltpu.VMEM((16, 6 * 256), F32),
        pltpu.VMEM((144, 6 * 256), BF16),
        pltpu.VMEM((144, 6 * 256), BF16),
        pltpu.VMEM((2, 512, 128), F32),
        pltpu.VMEM((16 * 16, 128), F32),
        pltpu.VMEM((C4, 128), BF16),
        pltpu.VMEM((N, 16, 128), BF16),
        pltpu.VMEM((C4, 128), BF16),
        pltpu.VMEM((N, 16, 128), BF16),
        pltpu.VMEM((CX, N * CR, C3), BF16),
        pltpu.VMEM((CX, N * CR, C4), BF16),
        pltpu.VMEM((C3, 2 * HALF), F32),
        pltpu.VMEM((N, 16, HALF), BF16),
        pltpu.VMEM((N, 16, HALF), BF16),
        pltpu.VMEM((256, C3), F32),
        pltpu.VMEM((N, 16, 512), BF16),
        pltpu.VMEM((N, 16, 512), BF16),
        pltpu.VMEM((N, 16, 256), BF16),
        pltpu.VMEM((N, 16, 256), BF16),
        pltpu.VMEM((N, 16, 128), BF16),
        pltpu.VMEM((N, 16, 128), BF16),
        pltpu.SemaphoreType.DMA((5,)),
        pltpu.SemaphoreType.DMA((2,)),
        pltpu.SemaphoreType.DMA((2,)),
        pltpu.SemaphoreType.DMA((4, 8)),
        pltpu.SemaphoreType.DMA((4, 8)),
        pltpu.SemaphoreType.DMA((8, N)),
        pltpu.SemaphoreType.DMA((8, N)),
    ]
    shapes = (
            jax.ShapeDtypeStruct((FX, FR, C3), BF16),
            jax.ShapeDtypeStruct((8 * 8, 27), F32),
            jax.ShapeDtypeStruct((8 * 16, 27), F32),
            jax.ShapeDtypeStruct((16 * 16, 27), F32),
    )
    results = pl.pallas_call(
        kernel,
        out_shape=shapes,
        in_specs=[hbm] * 5,
        out_specs=(vmem, vmem, vmem, vmem),
        scratch_shapes=scratch,
        compiler_params=pltpu.CompilerParams(
            collective_id=0, has_side_effects=True, vmem_limit_bytes=61 * 1024 * 1024
        ),
        name="unet_backward",
    )(
        features.reshape(FX, FR, C3),
        cotangent,
        weight_fine,
        weight_down,
        weight_mid,
    )
    out_feat, out_fine, out_down, out_mid = pl.pallas_call(
        hand_over,
        out_shape=shapes,
        in_specs=[vmem] * 4,
        out_specs=(vmem,) * 4,
        name="hand_over",
    )(*results)
    return (
        out_feat.reshape(FX, FX, FZ, C3),
        out_fine.reshape(8, 8, 27).transpose(0, 2, 1),
        out_down.reshape(8, 16, 27).transpose(0, 2, 1),
        out_mid.reshape(16, 16, 27).transpose(0, 2, 1),
    )


def solution(mesh):
    in_specs = (P("gx", "gy", None, None), P(), P(), P(), P("gx", "gy", None, None))
    out_specs = (
        P("gx", "gy", None, None),
        P("gx", None, "gy"),
        P("gx", None, "gy"),
        P("gx", None, "gy"),
    )
    return jax.shard_map(
        per_device, mesh=mesh, in_specs=in_specs, out_specs=out_specs, check_vma=False
    )
```
